256 devices in a mesh: fsdp: 64 (over z, x, core), rep: 4 (over y).
Axes of the slice: x: 4, y: 4, z: 8, core: 2. Of those that a mesh axis runs over, the one named last changes fastest.
Arguments:
- grads: bfloat16 [4, 3072, 18432], P('rep', 'fsdp'), may hold values from -0.59765625 to 0.59765625
- owner_map: int32 [4, 24], replicated, may hold values from 0 to 63, as said below
- stats_left: float32 [192, 768, 768], P('fsdp', 'rep'), may hold values from -1 to 8
- stats_right: float32 [192, 768, 768], P('fsdp', 'rep'), may hold values from -1 to 8
- roots_left: bfloat16 [192, 768, 768], P('fsdp', 'rep'), may hold values from -1 to 3, as said below
- roots_right: bfloat16 [192, 768, 768], P('fsdp', 'rep'), may hold values from -1 to 3, as said below
Outputs:
- new_left: float32 [192, 768, 768], P('fsdp', 'rep')
- new_right: float32 [192, 768, 768], P('fsdp', 'rep')
- update: bfloat16 [3072, 18432], P('fsdp')
The draws below stay inside these ranges and needn't reach their ends.
Inputs may be any that keep to these rules, and one draw needn't show every extreme that they name: `owner_map`: no owner holds more than 3 blocks, and some owner holds exactly 3; no owner holds more than 1 block of one block row, and some owner holds exactly 1 of one row. `roots_left`: each entry is a symmetric matrix. `roots_right`: each entry is a symmetric matrix.
All inputs are finite; a program needn't handle non-finite values.
Results may differ from the reference program's by a relative error of at most 0.017.
Values may be sent and summed in bfloat16 or wider, within the bound.
A program may use at most 128 MiB of HBM per device.

```python
import jax
import jax.numpy as jnp
from jax import lax

D = 3072
FF = 18432
B = 768
REPLICAS = 4
BROWS = 4
BCOLS = 24
BLOCKS = 96
SLOTS = 3
HELD = 192
N_FSDP = 64


def symmetric_fill(noise, diagonal):
    size = noise.shape[-1]
    rows = jnp.arange(size)[:, None]
    cols = jnp.arange(size)[None, :]
    identity = (rows == cols).astype(jnp.float32)
    mixed = 0.5 * (noise + jnp.swapaxes(noise, 1, 2))
    return mixed * (1.0 - identity) + diagonal[:, :, None] * identity


def draw_owner_map(key, part):
    key = jax.random.fold_in(key, 7)
    key_order, key_pick, key_shuffle = jax.random.split(key, 3)
    owner_order = jax.random.permutation(key_order, N_FSDP)
    remaining = SLOTS + jax.random.permutation(key_pick, N_FSDP * SLOTS - SLOTS)[:BLOCKS - SLOTS]
    chosen = jnp.concatenate([jnp.arange(SLOTS), remaining])
    tickets = jnp.sort(owner_order[chosen // SLOTS])
    ticket_table = tickets.reshape(BCOLS, BROWS).T
    shuffles = jax.vmap(lambda subkey: jax.random.permutation(subkey, BCOLS))(jax.random.split(key_shuffle, BROWS))
    return jnp.take_along_axis(ticket_table, shuffles, axis=1).astype(jnp.int32)


def stat_entries(key):
    key_noise, key_diag = jax.random.split(key)
    noise = 0.1 * jnp.clip(jax.random.normal(key_noise, (HELD, B, B), jnp.float32), -4.0, 4.0)
    diagonal = jax.random.uniform(key_diag, (HELD, B), jnp.float32, 1.0, 8.0)
    return symmetric_fill(noise, diagonal)


def root_entries(key):
    key_noise, key_diag = jax.random.split(key)
    spread = 0.85 / B ** 0.5
    noise = spread * jnp.clip(jax.random.normal(key_noise, (HELD, B, B), jnp.float32), -4.0, 4.0)
    diagonal = jax.random.uniform(key_diag, (HELD, B), jnp.float32, 1.5, 3.0)
    return symmetric_fill(noise, diagonal)


def draw_stats_left(key, part):
    key = jax.random.fold_in(key, 21)
    return stat_entries(key)


def draw_stats_right(key, part):
    key = jax.random.fold_in(key, 22)
    return stat_entries(key)


def draw_roots_left(key, part):
    key = jax.random.fold_in(key, 31)
    return root_entries(key).astype(jnp.bfloat16)


def draw_roots_right(key, part):
    key = jax.random.fold_in(key, 32)
    return root_entries(key).astype(jnp.bfloat16)


def block_levels(rng, extent, shards, low, high):
    factor_of, own = 1.0, jax.random.fold_in(rng, 6)
    for dim, shards_of in shards:
        steps = jnp.exp(jax.random.uniform(jax.random.fold_in(own, dim), (shards_of,), jnp.float32, low / len(shards), high / len(shards)))
        factor_of = factor_of * jnp.repeat(steps, extent[dim] // shards_of).reshape([-1 if axis == dim else 1 for axis in range(len(extent))])
    return factor_of


def normal_values(key, shape, width, reach, cuts=(), held_as=jnp.bfloat16):
    entries = jax.random.normal(key, shape, jnp.float32) * width
    if len(cuts) > 0:
        entries = block_levels(key, shape, cuts, -0.22, 0.18) * entries
    return jnp.clip(entries, min=-reach, max=reach).astype(held_as)


def setup_inputs(seed: int = 0) -> dict:
    key_of = jax.random.split(jax.random.key(seed), 7)
    grads = normal_values(key_of[0], (REPLICAS, D, FF), 0.1, 0.59765625, ((0, 4), (1, 64)))
    owner_map = draw_owner_map(jax.random.fold_in(key_of[6], 71), 0)
    stats_left = draw_stats_left(jax.random.fold_in(key_of[6], 71), 0)
    stats_right = draw_stats_right(jax.random.fold_in(key_of[6], 71), 0)
    roots_left = draw_roots_left(jax.random.fold_in(key_of[6], 71), 0)
    roots_right = draw_roots_right(jax.random.fold_in(key_of[6], 71), 0)
    return dict(grads=grads, owner_map=owner_map, stats_left=stats_left, stats_right=stats_right, roots_left=roots_left, roots_right=roots_right)


stat_decay = 0.95


def reference(grads, owner_map, stats_left, stats_right, roots_left, roots_right):
    summed = jnp.sum(grads.astype(jnp.float32), axis=0).astype(jnp.bfloat16)
    blocks = summed.reshape(BROWS, B, BCOLS, B).transpose(0, 2, 1, 3).reshape(BLOCKS, B, B)
    owners = owner_map.reshape(BLOCKS).astype(jnp.int32)
    position = jnp.arange(BLOCKS, dtype=jnp.int32)
    earlier = (owners[:, None] == owners[None, :]) & (position[None, :] < position[:, None])
    entry = (owners * SLOTS + jnp.sum(earlier.astype(jnp.int32), axis=1)).astype(jnp.int32)

    def one_block(inputs):
        block, index = inputs
        left_old = stats_left[index]
        right_old = stats_right[index]
        left_term = jnp.dot(block, block.T, preferred_element_type=jnp.float32)
        right_term = jnp.dot(block.T, block, preferred_element_type=jnp.float32)
        left_new = stat_decay * left_old + (1.0 - stat_decay) * left_term
        right_new = stat_decay * right_old + (1.0 - stat_decay) * right_term
        product = jnp.dot(roots_left[index], block, preferred_element_type=jnp.float32).astype(jnp.bfloat16)
        result = jnp.dot(product, roots_right[index], preferred_element_type=jnp.float32).astype(jnp.bfloat16)
        return left_new, right_new, result

    lefts, rights, results = lax.map(one_block, (blocks, entry))
    new_left = stats_left.at[entry].set(lefts)
    new_right = stats_right.at[entry].set(rights)
    update = results.reshape(BROWS, BCOLS, B, B).transpose(0, 2, 1, 3).reshape(D, FF)
    return new_left, new_right, update
```

```python
import jax
import jax.numpy as jnp
from jax import lax
from jax.experimental import pallas as pl
from jax.experimental.pallas import tpu as pltpu
from jax.sharding import PartitionSpec as P

stat_decay = 0.95
MESH = pl.DeviceIdType.MESH
LANES = 128
TALL = 48
PIECE = 80
BF16 = jnp.bfloat16
F32 = jnp.float32


def kernel(
    own, g_hbm, sl_hbm, sr_hbm, rl_hbm, rr_hbm,
    nl_hbm, nr_hbm, up_hbm,
    g_v, pk, rs_rel, rs_dir, rs_acc, rs_out, strip,
    out, ro, ri, rrel, turned, gi, G, GT,
    uo, rb, ag, to, ti, trel,
    sl_v, sr_v, rl_v, rr_v, up_v, jtbl, stbl,
    load_sem, copy_sem, store_sem, plane_sem, cube_sem,
    rs_s, rs_r, a_s, a_r, ro_s, ro_r, b_s, b_r, t_s, t_r, ag_s, ag_r,
):
    f = lax.axis_index("fsdp")
    q = lax.axis_index("rep")
    nf = lax.axis_size("fsdp")
    brows, bcols = own.shape
    group = nf // brows
    block = G.shape[0]
    slots, band, _ = sl_v.shape
    half = bcols // 2
    up, dn, opp = lax.rem(q + 1, 4), lax.rem(q + 3, 4), lax.rem(q + 2, 4)
    fi, fk = f // group, lax.rem(f, group)

    def rcopy(src, dst, ssem, rsem, rep):
        return pltpu.make_async_remote_copy(
            src_ref=src, dst_ref=dst, send_sem=ssem, recv_sem=rsem,
            device_id=(f, rep), device_id_type=MESH,
        )

    loads = [
        pltpu.make_async_copy(src, dst, load_sem.at[n])
        for n, (src, dst) in enumerate(
            [(g_hbm.at[0], g_v), (rl_hbm, rl_v), (rr_hbm, rr_v), (sl_hbm, sl_v), (sr_hbm, sr_v)]
        )
    ]
    for load in loads:
        load.start()

    def shift(o):
        return lax.rem(2 * lax.rem(o, 2) + lax.rem(o // 2, 4) + o // 8, 4)

    my_shift = shift(f)
    site_row = lax.rem(q + 4 - my_shift, 4)
    own_row = site_row == fi

    plane0 = (f // 8) * 8
    z_line = [(lax.rem(f + 8 * n, nf), q) for n in range(1, nf // 8)]
    x_line = [(plane0 + lax.rem(f + n, 8), q) for n in range(1, 8)]
    y_line = [(f, lax.rem(q + n, 4)) for n in range(1, 4)]

    def greet(sem, devices):
        for device in devices:
            pl.semaphore_signal(sem, inc=1, device_id=device, device_id_type=MESH)

    barrier = pltpu.get_barrier_semaphore()
    greet(barrier, y_line + x_line + z_line)

    def extra(t):
        return (0 if t < 2 else 16), 4 + t % 2

    loads[0].wait()

    def pack(j, carry):
        base = j * block
        for t in range(4):
            row, lane = extra(t)
            pk[t, j, 0:TALL, :] = g_v[:, pl.ds(pl.multiple_of(base + t * LANES, LANES), LANES)]
            pk[t, j, TALL:PIECE, :] = g_v[
                row : row + 32, pl.ds(pl.multiple_of(base + lane * LANES, LANES), LANES)
            ]
        return carry

    lax.fori_loop(0, bcols, pack, 0)
    pl.semaphore_wait(barrier, len(y_line) + len(x_line) + len(z_line))

    lo, hi = pl.ds(0, half), pl.ds(half, half)
    rs = [
        rcopy(pk.at[opp, lo], rs_rel.at[0], rs_s.at[0], rs_r.at[0], dn),
        rcopy(pk.at[opp, hi], rs_rel.at[1], rs_s.at[1], rs_r.at[1], up),
        rcopy(pk.at[up, lo], rs_dir.at[0], rs_s.at[2], rs_r.at[2], up),
        rcopy(pk.at[dn, hi], rs_dir.at[1], rs_s.at[3], rs_r.at[3], dn),
        rcopy(rs_out.at[0], rs_acc.at[0], rs_s.at[4], rs_r.at[4], dn),
        rcopy(rs_out.at[1], rs_acc.at[1], rs_s.at[5], rs_r.at[5], up),
    ]
    for copy in rs[:4]:
        copy.start()
    greet(plane_sem, x_line)

    def column_of(o, carry):
        col = jnp.int32(0)
        for j in range(bcols):
            col = jnp.where(own[fi, j] == o, jnp.int32(j), col)
        jtbl[o] = col
        return carry

    lax.fori_loop(0, nf, column_of, 0)
    held = []
    for t in range(brows):
        count = jnp.int32(0)
        for j in range(bcols):
            count = count + jnp.where(own[t, j] == f, jnp.int32(1), jnp.int32(0))
        held.append(count)
    before = jnp.int32(0)
    for t in range(brows):
        stbl[t] = jnp.minimum(before, slots - 1)
        before = before + held[t]
    slot_row, slot_valid = [], []
    for s in range(slots):
        row, valid = jnp.int32(0), jnp.int32(0)
        before = jnp.int32(0)
        for t in range(brows):
            hit = jnp.where(before == s, held[t], 0)
            row = row + hit * t
            valid = valid + hit
            before = before + held[t]
        slot_row.append(row)
        slot_valid.append(valid)

    loads[1].wait()
    loads[2].wait()
    for t in range(4):
        slot = stbl[lax.rem(t + 4 - my_shift, 4)]
        ro[t, 0] = rl_v[slot]
        ro[t, 1] = rr_v[slot]
    pl.semaphore_wait(plane_sem, len(x_line))
    greet(cube_sem, y_line)

    def relay_sum(n, first, target):
        def body(j, carry):
            rs_out[n, j] = (rs_rel[n, j].astype(F32) + pk[target, first + j].astype(F32)).astype(BF16)
            return carry

        lax.fori_loop(0, half, body, 0)

    rs[0].wait_recv()
    relay_sum(0, 0, dn)
    rs[4].start()
    rs[1].wait_recv()
    relay_sum(1, half, up)
    rs[5].start()

    def full_sum(n, first):
        def body(j, carry):
            strip[first + j] = (
                pk[q, first + j].astype(F32) + rs_dir[n, j].astype(F32) + rs_acc[n, j].astype(F32)
            ).astype(BF16)
            return carry

        lax.fori_loop(0, half, body, 0)

    rs[2].wait_recv()
    rs[4].wait_recv()
    full_sum(0, 0)
    rs[3].wait_recv()
    rs[5].wait_recv()
    full_sum(1, half)

    pl.semaphore_wait(cube_sem, len(y_line))

    def piece_copy(o):
        return pltpu.make_async_remote_copy(
            src_ref=out.at[o], dst_ref=gi.at[q, fk], send_sem=a_s, recv_sem=a_r,
            device_id=(o, lax.rem(fi + shift(o), 4)), device_id_type=MESH,
        )

    def send_piece(d, carry):
        o = lax.rem(f + d, nf)
        out[o] = strip[jtbl[o]]
        piece_copy(o).start()
        return carry

    lax.fori_loop(1, nf, send_piece, 0)

    @pl.when(own_row)
    def _():
        gi[q, fk] = strip[jtbl[f]]

    @pl.when(jnp.logical_not(own_row))
    def _():
        out[f] = strip[jtbl[f]]
        piece_copy(f).start()

    def await_pieces(sem):
        def some(count):
            view = out.at[pl.ds(0, count)]
            pltpu.make_async_copy(view, view, sem).wait()

        pl.when(own_row)(lambda: some(nf - 1))
        pl.when(jnp.logical_not(own_row))(lambda: some(nf))

    def exchange(far, outs, ins, far_ins, rel, ssem, rsem):
        return [
            rcopy(far[0], rel.at[0], ssem.at[0], rsem.at[0], dn),
            rcopy(far[1], rel.at[1], ssem.at[1], rsem.at[1], up),
            rcopy(outs.at[up], ins.at[q], ssem.at[2], rsem.at[2], up),
            rcopy(outs.at[dn], ins.at[q], ssem.at[3], rsem.at[3], dn),
            rcopy(rel.at[0], far_ins[0], ssem.at[4], rsem.at[4], dn),
            rcopy(rel.at[1], far_ins[1], ssem.at[5], rsem.at[5], up),
        ]

    def begin(copies, own_copy):
        for copy in copies[:4]:
            copy.start()
        own_copy.start()

    def forward(copies):
        copies[0].wait_recv()
        copies[4].start()
        copies[1].wait_recv()
        copies[5].start()

    def finish(copies, own_copy):
        for copy in copies[2:]:
            copy.wait_recv()
        own_copy.wait()

    def window(t):
        return pl.ds(pl.multiple_of(LANES * (t + t // 2), LANES), 2 * LANES)

    roots = exchange(
        [ro.at[opp, n, :, window(q)] for n in range(2)], ro, ri,
        [ri.at[up, 0, :, window(up)], ri.at[dn, 1, :, window(dn)]], rrel, ro_s, ro_r,
    )
    roots_own = pltpu.make_async_copy(ro.at[q], ri.at[q], copy_sem.at[0])
    begin(roots, roots_own)
    forward(roots)
    finish(roots, roots_own)
    for n in range(2):
        turned[...] = ri[:, n, :, window(opp)].reshape(block, 2 * LANES).T
        ri[opp, n] = turned[pl.ds(pl.multiple_of(64 * lax.rem(opp, 2), 16), band), :]

    await_pieces(a_r)

    def unpack_block(k, carry):
        row0 = pl.multiple_of(k * TALL, 16)
        for t in range(4):
            row, lane = extra(t)
            G[pl.ds(row0, TALL), t * LANES : (t + 1) * LANES] = gi[t, k, 0:TALL, :]
            skip = 0 if t < 2 else 16
            G[pl.ds(pl.multiple_of(row0 + row + skip, 16), 32 - skip), lane * LANES : (lane + 1) * LANES] = gi[
                t, k, TALL + skip : PIECE, :
            ]
        return carry

    lax.fori_loop(0, group, unpack_block, 0)

    per_band = band // TALL

    def precondition(c, carry):
        p = jnp.dot(ri[c, 0], G[...], preferred_element_type=F32).astype(BF16)
        u = jnp.dot(p, ri[:, 1].reshape(block, block), preferred_element_type=F32).astype(BF16)
        for n in range(per_band):
            k = c * per_band + n
            for t in range(4):
                row, lane = extra(t)
                uo[t, k, 0:TALL, :] = u[n * TALL : (n + 1) * TALL, t * LANES : (t + 1) * LANES]
                uo[t, k, TALL:PIECE, :] = u[
                    n * TALL + row : n * TALL + row + 32, lane * LANES : (lane + 1) * LANES
                ]
        return carry

    lax.fori_loop(0, 4, precondition, 0)

    def piece_back(e):
        t, k = lax.rem(e, 4), lax.rem(e // 4 + fk, group)
        p = site_row * group + k
        copy = pltpu.make_async_remote_copy(
            src_ref=uo.at[t, k], dst_ref=rb.at[f], send_sem=b_s, recv_sem=b_r,
            device_id=(p, t), device_id_type=MESH,
        )
        return copy, jnp.logical_and(p == f, t == q)

    def send_back(e, carry):
        copy, here = piece_back(e)

        @pl.when(jnp.logical_not(here))
        def _():
            copy.start()

        return carry

    lax.fori_loop(0, nf, send_back, 0)

    @pl.when(own_row)
    def _():
        rb[f] = uo[q, fk]

    GT[...] = G[...].T

    def products_left(c, carry):
        rows = G[pl.ds(pl.multiple_of(c * band, 16), band), :]
        to[c, 0] = lax.dot_general(
            rows, G[...], (((1,), (1,)), ((), ())), preferred_element_type=F32
        ).astype(BF16)
        return carry

    def products_right(c, carry):
        rows = GT[pl.ds(pl.multiple_of(c * band, 16), band), :]
        to[c, 1] = jnp.dot(rows, G[...], preferred_element_type=F32).astype(BF16)
        return carry

    lax.fori_loop(0, 4, products_left, 0)
    lax.fori_loop(0, 4, products_right, 0)

    stats = exchange(
        [to.at[opp, 0], to.at[opp, 1]], to, ti, [ti.at[up, 0], ti.at[dn, 1]], trel, t_s, t_r
    )
    stats_own = pltpu.make_async_copy(to.at[q], ti.at[q], copy_sem.at[1])
    begin(stats, stats_own)
    forward(stats)
    finish(stats, stats_own)
    loads[3].wait()
    loads[4].wait()
    for s in range(slots):
        for n, ref in ((0, sl_v), (1, sr_v)):
            old = ref[s]
            term = ti[lax.rem(slot_row[s] + my_shift, 4), n].astype(F32)
            ref[s] = jnp.where(slot_valid[s] > 0, stat_decay * old + (1.0 - stat_decay) * term, old)
    stores = [
        pltpu.make_async_copy(sl_v, nl_hbm, store_sem.at[0]),
        pltpu.make_async_copy(sr_v, nr_hbm, store_sem.at[1]),
        pltpu.make_async_copy(up_v, up_hbm, store_sem.at[2]),
    ]
    stores[0].start()
    stores[1].start()

    await_pieces(b_r)

    def pick(j, carry):
        ag[q, j] = rb[own[fi, j]]
        return carry

    lax.fori_loop(0, bcols, pick, 0)
    gather = [
        rcopy(ag.at[q], ag.at[q], ag_s.at[0], ag_r.at[0], up),
        rcopy(ag.at[q], ag.at[q], ag_s.at[1], ag_r.at[1], dn),
        rcopy(ag.at[up, lo], ag.at[up, lo], ag_s.at[2], ag_r.at[2], dn),
        rcopy(ag.at[dn, hi], ag.at[dn, hi], ag_s.at[3], ag_r.at[3], up),
    ]
    gather[0].start()
    gather[1].start()
    gather[1].wait_recv()
    gather[2].start()
    gather[0].wait_recv()
    gather[3].start()
    gather[2].wait_recv()
    gather[3].wait_recv()

    def unpack_row(j, carry):
        base = j * block
        for t in range(4):
            row, lane = extra(t)
            skip = 0 if t < 2 else 16
            up_v[:, pl.ds(pl.multiple_of(base + t * LANES, LANES), LANES)] = ag[t, j, 0:TALL, :]
            up_v[row + skip : row + 32, pl.ds(pl.multiple_of(base + lane * LANES, LANES), LANES)] = ag[
                t, j, TALL + skip : PIECE, :
            ]
        return carry

    lax.fori_loop(0, bcols, unpack_row, 0)
    stores[2].start()

    for copies in (rs, roots, stats, gather):
        for copy in copies:
            copy.wait_send()
    await_pieces(a_s)
    await_pieces(b_s)
    for store in stores:
        store.wait()


def shards(grads, owner_map, stats_left, stats_right, roots_left, roots_right):
    _, rows, width = grads.shape
    slots, band, block = stats_left.shape
    brows, bcols = owner_map.shape
    nf = lax.axis_size("fsdp")
    group = nf // brows
    half = bcols // 2
    dma, reg = pltpu.SemaphoreType.DMA, pltpu.VMEM
    msg = (PIECE, LANES)
    scratch = [
        reg((rows, width), BF16),
        reg((4, bcols) + msg, BF16),
        reg((2, half) + msg, BF16),
        reg((2, half) + msg, BF16),
        reg((2, half) + msg, BF16),
        reg((2, half) + msg, BF16),
        reg((bcols,) + msg, BF16),
        reg((nf,) + msg, BF16),
        reg((4, 2, band, block), BF16),
        reg((4, 2, band, block), BF16),
        reg((2, band, 2 * LANES), BF16),
        reg((2 * LANES, block), BF16),
        reg((4, group) + msg, BF16),
        reg((block, block), BF16),
        reg((block, block), BF16),
        reg((4, group) + msg, BF16),
        reg((nf,) + msg, BF16),
        reg((4, bcols) + msg, BF16),
        reg((4, 2, band, block), BF16),
        reg((4, 2, band, block), BF16),
        reg((2, band, block), BF16),
        reg((slots, band, block), F32),
        reg((slots, band, block), F32),
        reg((slots, band, block), BF16),
        reg((slots, band, block), BF16),
        reg((rows, width), BF16),
        pltpu.SMEM((nf,), jnp.int32),
        pltpu.SMEM((brows,), jnp.int32),
        dma((5,)), dma((2,)), dma((3,)), pltpu.SemaphoreType.REGULAR, pltpu.SemaphoreType.REGULAR,
        dma((6,)), dma((6,)), dma, dma, dma((6,)), dma((6,)),
        dma, dma, dma((6,)), dma((6,)), dma((4,)), dma((4,)),
    ]
    hbm = pl.BlockSpec(memory_space=pl.ANY)
    return pl.pallas_call(
        kernel,
        out_shape=(
            jax.ShapeDtypeStruct(stats_left.shape, F32),
            jax.ShapeDtypeStruct(stats_right.shape, F32),
            jax.ShapeDtypeStruct((rows, width), BF16),
        ),
        in_specs=[pl.BlockSpec(memory_space=pltpu.SMEM)] + [hbm] * 5,
        out_specs=(hbm, hbm, hbm),
        scratch_shapes=scratch,
        compiler_params=pltpu.CompilerParams(
            collective_id=0, has_side_effects=True, vmem_limit_bytes=60 * 1024 * 1024
        ),
        name="shampoo",
    )(owner_map, grads, stats_left, stats_right, roots_left, roots_right)


def solution(mesh):
    in_specs = (
        P("rep", "fsdp", None),
        P(),
        P("fsdp", "rep", None),
        P("fsdp", "rep", None),
        P("fsdp", "rep", None),
        P("fsdp", "rep", None),
    )
    out_specs = (P("fsdp", "rep", None), P("fsdp", "rep", None), P("fsdp", None))
    return jax.shard_map(shards, mesh=mesh, in_specs=in_specs, out_specs=out_specs, check_vma=False)
```

```python
import jax
import jax.numpy as jnp
from jax import lax
from jax.experimental import pallas as pl
from jax.experimental.pallas import tpu as pltpu
from jax.sharding import PartitionSpec as P

stat_decay = 0.95
MESH = pl.DeviceIdType.MESH
LANES = 128
TALL = 48
PIECE = 80
CHUNKS = ((0, 32), (32, 32), (64, 16))
BF16 = jnp.bfloat16
F32 = jnp.float32


class Copy:
    def __init__(self, copy, sends=None, receives=None):
        self.copy, self.sends, self.receives = copy, sends, receives

    def start(self):
        gated(self.sends, self.copy.start)

    def wait_send(self):
        gated(self.sends, self.copy.wait_send)

    def wait_recv(self):
        gated(self.receives, self.copy.wait_recv)


def gated(condition, act):
    if condition is None:
        act()
    else:

        @pl.when(condition)
        def _():
            act()


def kernel(
    own, g_hbm, sl_hbm, sr_hbm, rl_hbm, rr_hbm,
    nl_hbm, nr_hbm, up_hbm,
    g_v, pk, rs_rel, rs_dir, rs_acc, rs_out, strip,
    out, ro, ri, rrel, turned, gi, G, GT,
    uo, rb0, rb1, rb2, ag, to, ti, trel,
    sl_v, sr_v, rl_v, rr_v, up_v, jtbl, stbl,
    load_sem, copy_sem, store_sem, near_sem, line_sem, plane_sem, cube_sem,
    rs_s, rs_r, a_s, a_r, ro_s, ro_r, b_s, b_r, t_s, t_r, ag_s, ag_r,
):
    f = lax.axis_index("fsdp")
    q = lax.axis_index("rep")
    nf = lax.axis_size("fsdp")
    brows, bcols = own.shape
    group = nf // brows
    block = G.shape[0]
    slots, band, _ = sl_v.shape
    half = bcols // 2
    up, dn, opp = lax.rem(q + 1, 4), lax.rem(q + 3, 4), lax.rem(q + 2, 4)
    fi, fk, core = f // group, lax.rem(f, group), lax.rem(f, 2)

    def rcopy(src, dst, ssem, rsem, rep, sends=None, receives=None):
        copy = pltpu.make_async_remote_copy(
            src_ref=src, dst_ref=dst, send_sem=ssem, recv_sem=rsem,
            device_id=(f, rep), device_id_type=MESH,
        )
        return Copy(copy, sends, receives)

    loads = [
        pltpu.make_async_copy(src, dst, load_sem.at[n])
        for n, (src, dst) in enumerate(
            [(g_hbm.at[0], g_v), (rl_hbm, rl_v), (rr_hbm, rr_v), (sl_hbm, sl_v), (sr_hbm, sr_v)]
        )
    ]

    def shift(o):
        return lax.rem(2 * lax.rem(o, 2) + lax.rem(o // 2, 4) + o // 8, 4)

    my_shift = shift(f)
    site_row = lax.rem(q + 4 - my_shift, 4)
    own_row = site_row == fi

    def along_z(n):
        return (lax.rem(f + 8 * n, nf), q)

    def along_x(n):
        return ((f // 8) * 8 + lax.rem(f + n, 8), q)

    near = [along_z(1), along_z(7), along_x(1), along_x(7)]
    further = [along_z(2), along_z(6), along_x(2), along_x(6)]
    x_line = [along_x(n) for n in range(1, 8)]
    y_line = [(f, up), (f, dn), (f, opp)]

    def greet(sem, devices):
        for device in devices:
            pl.semaphore_signal(sem, inc=1, device_id=device, device_id_type=MESH)

    loads[0].start()
    barrier = pltpu.get_barrier_semaphore()
    greet(barrier, y_line + near)
    for load in loads[1:]:
        load.start()

    def column_of(o, carry):
        col = jnp.int32(0)
        for j in range(bcols):
            col = jnp.where(own[fi, j] == o, jnp.int32(j), col)
        jtbl[o] = col
        return carry

    lax.fori_loop(0, nf, column_of, 0)
    held = []
    for t in range(brows):
        count = jnp.int32(0)
        for j in range(bcols):
            count = count + jnp.where(own[t, j] == f, jnp.int32(1), jnp.int32(0))
        held.append(count)
    before = jnp.int32(0)
    for t in range(brows):
        stbl[t] = jnp.minimum(before, slots - 1)
        before = before + held[t]
    slot_row, slot_valid = [], []
    for s in range(slots):
        row, valid = jnp.int32(0), jnp.int32(0)
        before = jnp.int32(0)
        for t in range(brows):
            hit = jnp.where(before == s, held[t], 0)
            row = row + hit * t
            valid = valid + hit
            before = before + held[t]
        slot_row.append(row)
        slot_valid.append(valid)

    def tall(t, c):
        return lax.rem(t + 2 * c, 4) < 2

    tall_q, tall_up, tall_dn, tall_opp = [tall(t, core) for t in (q, up, dn, opp)]

    def lanes(base, group_of):
        return pl.ds(pl.multiple_of(base + group_of * LANES, LANES), LANES)

    loads[0].wait()

    def pack(j, carry):
        base = j * block
        for t in range(4):
            pk[t, j, 0:TALL, :] = g_v[:, lanes(base, t)]
        for t in range(2):
            pk[t + 2 * core, j, TALL:PIECE, :] = g_v[0:32, lanes(base, 4 + t)]
            pk[t + 2 * (1 - core), j, TALL:64, :] = g_v[32:TALL, lanes(base, 4 + t)]
        return carry

    lax.fori_loop(0, bcols, pack, 0)
    pl.semaphore_wait(barrier, len(y_line) + len(near))

    def sums(n):
        row, count = CHUNKS[n]
        lo, hi, rows = pl.ds(0, half), pl.ds(half, half), pl.ds(row, count)
        if n < 2:
            s_up = s_dn = s_opp = r_up = r_dn = r_q = None
        else:
            s_up, s_dn, s_opp, r_up, r_dn, r_q = tall_up, tall_dn, tall_opp, tall_up, tall_dn, tall_q
        ss, rr = rs_s.at[n], rs_r.at[n]
        return [
            rcopy(pk.at[opp, lo, rows], rs_rel.at[0, :, rows], ss.at[0], rr.at[0], dn, s_opp, r_dn),
            rcopy(pk.at[opp, hi, rows], rs_rel.at[1, :, rows], ss.at[1], rr.at[1], up, s_opp, r_up),
            rcopy(pk.at[up, lo, rows], rs_dir.at[0, :, rows], ss.at[2], rr.at[2], up, s_up, r_q),
            rcopy(pk.at[dn, hi, rows], rs_dir.at[1, :, rows], ss.at[3], rr.at[3], dn, s_dn, r_q),
            rcopy(rs_out.at[0, :, rows], rs_acc.at[0, :, rows], ss.at[4], rr.at[4], dn, s_dn, r_q),
            rcopy(rs_out.at[1, :, rows], rs_acc.at[1, :, rows], ss.at[5], rr.at[5], up, s_up, r_q),
        ]

    rs = [sums(n) for n in range(3)]

    def first_sends(n):
        for copy in rs[n][:4]:
            copy.start()

    def relay_sums(n):
        row, count = CHUNKS[n]
        rows = slice(row, row + count)
        for side, first, target in ((0, 0, dn), (1, half, up)):
            rs[n][side].wait_recv()

            def body(j, carry):
                total = rs_rel[side, j, rows].astype(F32) + pk[target, first + j, rows].astype(F32)
                rs_out[side, j, rows] = total.astype(BF16)
                return carry

            lax.fori_loop(0, half, body, 0)
            rs[n][4 + side].start()

    def full_sums(n):
        row, count = CHUNKS[n]
        rows = slice(row, row + count)
        for side, first in ((0, 0), (1, half)):
            rs[n][2 + side].wait_recv()
            rs[n][4 + side].wait_recv()

            def body(j, carry):
                total = pk[q, first + j, rows].astype(F32) + rs_dir[side, j, rows].astype(F32)
                strip[first + j, rows] = (total + rs_acc[side, j, rows].astype(F32)).astype(BF16)
                return carry

            lax.fori_loop(0, half, body, 0)

    def send_pieces(n):
        row, count = CHUNKS[n]
        rows = pl.ds(row, count)

        def piece_copy(o):
            return pltpu.make_async_remote_copy(
                src_ref=out.at[o, rows], dst_ref=gi.at[q, fk, rows], send_sem=a_s.at[n], recv_sem=a_r.at[n],
                device_id=(o, lax.rem(fi + shift(o), 4)), device_id_type=MESH,
            )

        def send_piece(d, carry):
            o = lax.rem(f + d, nf)
            out[o, row : row + count] = strip[jtbl[o], row : row + count]
            piece_copy(o).start()
            return carry

        def send_all():
            lax.fori_loop(1, nf, send_piece, 0)

            @pl.when(own_row)
            def _():
                gi[q, fk, row : row + count] = strip[jtbl[f], row : row + count]

            @pl.when(jnp.logical_not(own_row))
            def _():
                out[f, row : row + count] = strip[jtbl[f], row : row + count]
                piece_copy(f).start()

        gated(None if n < 2 else tall_q, send_all)

    def await_pieces(sem, n, total, here):
        count = CHUNKS[n][1]

        def some(pieces):
            view = out.at[pl.ds(0, pieces), pl.ds(0, count)]
            pltpu.make_async_copy(view, view, sem.at[n]).wait()

        pl.when(here)(lambda: some(total - 1))
        pl.when(jnp.logical_not(here))(lambda: some(total))

    def await_strip(sem, n):
        gated(None if n < 2 else tall_q, lambda: await_pieces(sem, n, nf, own_row))

    def await_block(sem, n):
        if n < 2:
            await_pieces(sem, n, nf, own_row)
        else:
            await_pieces(sem, n, nf // 2, jnp.logical_and(own_row, tall_q))

    def exchange(far, outs, ins, far_ins, rel, ssem, rsem):
        return [
            rcopy(far[0], rel.at[0], ssem.at[0], rsem.at[0], dn),
            rcopy(far[1], rel.at[1], ssem.at[1], rsem.at[1], up),
            rcopy(outs.at[up], ins.at[q], ssem.at[2], rsem.at[2], up),
            rcopy(outs.at[dn], ins.at[q], ssem.at[3], rsem.at[3], dn),
            rcopy(rel.at[0], far_ins[0], ssem.at[4], rsem.at[4], dn),
            rcopy(rel.at[1], far_ins[1], ssem.at[5], rsem.at[5], up),
        ]

    def begin(copies, own_copy):
        for copy in copies[:4]:
            copy.start()
        own_copy.start()

    def forward(copies):
        copies[0].wait_recv()
        copies[4].start()
        copies[1].wait_recv()
        copies[5].start()

    def finish(copies, own_copy):
        for copy in copies[2:]:
            copy.wait_recv()
        own_copy.wait()

    def window(t):
        return pl.ds(pl.multiple_of(LANES * (t + t // 2), LANES), 2 * LANES)

    roots = exchange(
        [ro.at[opp, n, :, window(q)] for n in range(2)], ro, ri,
        [ri.at[up, 0, :, window(up)], ri.at[dn, 1, :, window(dn)]], rrel, ro_s, ro_r,
    )
    roots_own = pltpu.make_async_copy(ro.at[q], ri.at[q], copy_sem.at[0])

    first_sends(0)
    greet(near_sem, near)
    first_sends(1)
    pl.semaphore_wait(near_sem, len(near))
    greet(line_sem, further)
    loads[1].wait()
    loads[2].wait()
    for t in range(4):
        slot = stbl[lax.rem(t + 4 - my_shift, 4)]
        ro[t, 0] = rl_v[slot]
        ro[t, 1] = rr_v[slot]
    pl.semaphore_wait(line_sem, len(further))
    greet(plane_sem, x_line)
    relay_sums(0)
    first_sends(2)
    pl.semaphore_wait(plane_sem, len(x_line))
    greet(cube_sem, y_line)
    relay_sums(1)
    full_sums(0)
    pl.semaphore_wait(cube_sem, len(y_line))
    send_pieces(0)
    relay_sums(2)
    begin(roots, roots_own)
    full_sums(1)
    send_pieces(1)
    full_sums(2)
    send_pieces(2)
    forward(roots)
    finish(roots, roots_own)
    for n in range(2):
        turned[...] = ri[:, n, :, window(opp)].reshape(block, 2 * LANES).T
        ri[opp, n] = turned[pl.ds(pl.multiple_of(64 * lax.rem(opp, 2), 16), band), :]

    for n in range(3):
        await_block(a_r, n)

    def unpack_block(k, carry):
        c = lax.rem(k, 2)
        row0 = pl.multiple_of(k * TALL, 16)
        for t in range(4):
            G[pl.ds(row0, TALL), t * LANES : (t + 1) * LANES] = gi[t, k, 0:TALL, :]
        for t in range(2):
            into = slice((4 + t) * LANES, (5 + t) * LANES)
            G[pl.ds(row0, 32), into] = gi[t + 2 * c, k, TALL:PIECE, :]
            G[pl.ds(pl.multiple_of(row0 + 32, 16), 16), into] = gi[t + 2 * (1 - c), k, TALL:64, :]
        return carry

    lax.fori_loop(0, group, unpack_block, 0)

    per_band = band // TALL

    def precondition(b, carry):
        p = jnp.dot(ri[b, 0], G[...], preferred_element_type=F32).astype(BF16)
        u = jnp.dot(p, ri[:, 1].reshape(block, block), preferred_element_type=F32).astype(BF16)
        for n in range(per_band):
            k = b * per_band + n
            row0, c = n * TALL, n % 2
            for t in range(4):
                uo[t, k, 0:TALL, :] = u[row0 : row0 + TALL, t * LANES : (t + 1) * LANES]
            for t in range(2):
                part = u[row0 : row0 + TALL, (4 + t) * LANES : (5 + t) * LANES]
                uo[t + 2 * c, k, TALL:PIECE, :] = part[0:32]
                uo[t + 2 * (1 - c), k, TALL:64, :] = part[32:TALL]
        return carry

    lax.fori_loop(0, 4, precondition, 0)

    rb = (rb0, rb1, rb2)

    def send_back(n):
        row, count = CHUNKS[n]
        rows = pl.ds(row, count)

        def one(e, carry):
            if n < 2:
                t, k = lax.rem(e, 4), lax.rem(e // 4 + fk, group)
            else:
                k = lax.rem(e // 2 + fk, group)
                t = 2 * lax.rem(k, 2) + lax.rem(e, 2)
            p = site_row * group + k
            copy = pltpu.make_async_remote_copy(
                src_ref=uo.at[t, k, rows], dst_ref=rb[n].at[f], send_sem=b_s.at[n], recv_sem=b_r.at[n],
                device_id=(p, t), device_id_type=MESH,
            )

            @pl.when(jnp.logical_not(jnp.logical_and(p == f, t == q)))
            def _():
                copy.start()

            return carry

        lax.fori_loop(0, nf if n < 2 else nf // 2, one, 0)

        @pl.when(own_row)
        def _():
            rb[n][f] = uo[q, fk, row : row + count]

    for n in range(3):
        send_back(n)

    GT[...] = G[...].T

    def products_left(c, carry):
        rows = G[pl.ds(pl.multiple_of(c * band, 16), band), :]
        to[c, 0] = lax.dot_general(
            rows, G[...], (((1,), (1,)), ((), ())), preferred_element_type=F32
        ).astype(BF16)
        return carry

    def products_right(c, carry):
        rows = GT[pl.ds(pl.multiple_of(c * band, 16), band), :]
        to[c, 1] = jnp.dot(rows, G[...], preferred_element_type=F32).astype(BF16)
        return carry

    lax.fori_loop(0, 4, products_left, 0)
    lax.fori_loop(0, 4, products_right, 0)

    stats = exchange(
        [to.at[opp, 0], to.at[opp, 1]], to, ti, [ti.at[up, 0], ti.at[dn, 1]], trel, t_s, t_r
    )
    stats_own = pltpu.make_async_copy(to.at[q], ti.at[q], copy_sem.at[1])
    begin(stats, stats_own)
    forward(stats)

    def spread(n):
        row, count = CHUNKS[n]
        lo, hi, rows = pl.ds(0, half), pl.ds(half, half), pl.ds(row, count)
        if n < 2:
            t_q = t_up = t_dn = t_opp = None
        else:
            t_q, t_up, t_dn, t_opp = tall_q, tall_up, tall_dn, tall_opp
        ss, rr = ag_s.at[n], ag_r.at[n]
        mine = ag.at[q, :, rows]
        from_up, from_dn = ag.at[up, lo, rows], ag.at[dn, hi, rows]
        return [
            rcopy(mine, mine, ss.at[0], rr.at[0], up, t_q, t_dn),
            rcopy(mine, mine, ss.at[1], rr.at[1], dn, t_q, t_up),
            rcopy(from_up, from_up, ss.at[2], rr.at[2], dn, t_up, t_opp),
            rcopy(from_dn, from_dn, ss.at[3], rr.at[3], up, t_dn, t_opp),
        ]

    gather = [spread(n) for n in range(3)]

    def start_gather(n):
        row, count = CHUNKS[n]
        await_strip(b_r, n)

        def pick(j, carry):
            ag[q, j, row : row + count] = rb[n][own[fi, j]]
            return carry

        lax.fori_loop(0, bcols, pick, 0)
        gather[n][0].start()
        gather[n][1].start()

    def forward_gather(n):
        gather[n][1].wait_recv()
        gather[n][2].start()
        gather[n][0].wait_recv()
        gather[n][3].start()

    start_gather(0)
    start_gather(1)
    forward_gather(0)
    start_gather(2)
    forward_gather(1)
    forward_gather(2)

    finish(stats, stats_own)
    loads[3].wait()
    loads[4].wait()
    for s in range(slots):
        for n, ref in ((0, sl_v), (1, sr_v)):
            old = ref[s]
            term = ti[lax.rem(slot_row[s] + my_shift, 4), n].astype(F32)
            ref[s] = jnp.where(slot_valid[s] > 0, stat_decay * old + (1.0 - stat_decay) * term, old)
    stores = [
        pltpu.make_async_copy(sl_v, nl_hbm, store_sem.at[0]),
        pltpu.make_async_copy(sr_v, nr_hbm, store_sem.at[1]),
    ] + [
        pltpu.make_async_copy(up_v.at[pl.ds(row, 16)], up_hbm.at[pl.ds(row, 16)], store_sem.at[2 + n])
        for n, row in enumerate((0, 32, 16))
    ]
    stores[0].start()
    stores[1].start()

    def finish_gather(n):
        gather[n][2].wait_recv()
        gather[n][3].wait_recv()

        def unpack_row(j, carry):
            base = j * block
            if n == 0:
                for t in range(4):
                    up_v[0:32, lanes(base, t)] = ag[t, j, 0:32, :]
            elif n == 1:
                for t in range(4):
                    up_v[32:TALL, lanes(base, t)] = ag[t, j, 32:TALL, :]
                for t in range(2):
                    up_v[0:16, lanes(base, 4 + t)] = ag[t + 2 * core, j, TALL:64, :]
                    up_v[32:TALL, lanes(base, 4 + t)] = ag[t + 2 * (1 - core), j, TALL:64, :]
            else:
                for t in range(2):
                    up_v[16:32, lanes(base, 4 + t)] = ag[t + 2 * core, j, 64:PIECE, :]
            return carry

        lax.fori_loop(0, bcols, unpack_row, 0)

    finish_gather(0)
    finish_gather(1)
    stores[2].start()
    stores[3].start()
    finish_gather(2)
    stores[4].start()

    for copies in rs + [roots, stats] + gather:
        for copy in copies:
            copy.wait_send()
    for n in range(3):
        await_strip(a_s, n)
        await_block(b_s, n)
    for store in stores:
        store.wait()


def shards(grads, owner_map, stats_left, stats_right, roots_left, roots_right):
    _, rows, width = grads.shape
    slots, band, block = stats_left.shape
    brows, bcols = owner_map.shape
    nf = lax.axis_size("fsdp")
    group = nf // brows
    half = bcols // 2
    dma, count, reg = pltpu.SemaphoreType.DMA, pltpu.SemaphoreType.REGULAR, pltpu.VMEM
    msg = (PIECE, LANES)
    scratch = [
        reg((rows, width), BF16),
        reg((4, bcols) + msg, BF16),
        reg((2, half) + msg, BF16),
        reg((2, half) + msg, BF16),
        reg((2, half) + msg, BF16),
        reg((2, half) + msg, BF16),
        reg((bcols,) + msg, BF16),
        reg((nf,) + msg, BF16),
        reg((4, 2, band, block), BF16),
        reg((4, 2, band, block), BF16),
        reg((2, band, 2 * LANES), BF16),
        reg((2 * LANES, block), BF16),
        reg((4, group) + msg, BF16),
        reg((block, block), BF16),
        reg((block, block), BF16),
        reg((4, group) + msg, BF16),
        reg((nf, 32, LANES), BF16),
        reg((nf, 32, LANES), BF16),
        reg((nf, 16, LANES), BF16),
        reg((4, bcols) + msg, BF16),
        reg((4, 2, band, block), BF16),
        reg((4, 2, band, block), BF16),
        reg((2, band, block), BF16),
        reg((slots, band, block), F32),
        reg((slots, band, block), F32),
        reg((slots, band, block), BF16),
        reg((slots, band, block), BF16),
        reg((rows, width), BF16),
        pltpu.SMEM((nf,), jnp.int32),
        pltpu.SMEM((brows,), jnp.int32),
        dma((5,)), dma((2,)), dma((5,)), count, count, count, count,
        dma((3, 6)), dma((3, 6)), dma((3,)), dma((3,)), dma((6,)), dma((6,)),
        dma((3,)), dma((3,)), dma((6,)), dma((6,)), dma((3, 4)), dma((3, 4)),
    ]
    hbm = pl.BlockSpec(memory_space=pl.ANY)
    return pl.pallas_call(
        kernel,
        out_shape=(
            jax.ShapeDtypeStruct(stats_left.shape, F32),
            jax.ShapeDtypeStruct(stats_right.shape, F32),
            jax.ShapeDtypeStruct((rows, width), BF16),
        ),
        in_specs=[pl.BlockSpec(memory_space=pltpu.SMEM)] + [hbm] * 5,
        out_specs=(hbm, hbm, hbm),
        scratch_shapes=scratch,
        compiler_params=pltpu.CompilerParams(
            collective_id=0, has_side_effects=True, vmem_limit_bytes=60 * 1024 * 1024
        ),
        name="shampoo",
    )(owner_map, grads, stats_left, stats_right, roots_left, roots_right)


def solution(mesh):
    in_specs = (
        P("rep", "fsdp", None),
        P(),
        P("fsdp", "rep", None),
        P("fsdp", "rep", None),
        P("fsdp", "rep", None),
        P("fsdp", "rep", None),
    )
    out_specs = (P("fsdp", "rep", None), P("fsdp", "rep", None), P("fsdp", None))
    return jax.shard_map(shards, mesh=mesh, in_specs=in_specs, out_specs=out_specs, check_vma=False)
```

```python
import jax
import jax.numpy as jnp
from jax import lax
from jax.experimental import pallas as pl
from jax.experimental.pallas import tpu as pltpu
from jax.sharding import PartitionSpec as P

stat_decay = 0.95
MESH = pl.DeviceIdType.MESH
LANES = 128
TALL = 48
PIECE = 80
CHUNKS = ((0, 32), (32, 32), (64, 16))
BF16 = jnp.bfloat16
F32 = jnp.float32


class Copy:
    def __init__(self, copy, sends=None, receives=None):
        self.copy, self.sends, self.receives = copy, sends, receives

    def start(self):
        gated(self.sends, self.copy.start)

    def wait_send(self):
        gated(self.sends, self.copy.wait_send)

    def wait_recv(self):
        gated(self.receives, self.copy.wait_recv)


def gated(condition, act):
    if condition is None:
        act()
    else:

        @pl.when(condition)
        def _():
            act()


def kernel(
    own, g_hbm, rl_hbm, rr_hbm,
    decay, terms_hbm, up_hbm,
    g_v, pk, rs_rel, rs_dir, rs_acc, rs_out, strip,
    out, ro, ri, turned, gi, G, GT,
    uo, rb0, rb1, rb2, ag, to, ti, terms,
    rl_v, rr_v, up_v, jtbl, stbl,
    load_sem, copy_sem, store_sem, near_sem, line_sem, plane_sem, cube_sem,
    rs_s, rs_r, a_s, a_r, ro_s, ro_r, b_s, b_r, t_s, t_r, ag_s, ag_r,
):
    f = lax.axis_index("fsdp")
    q = lax.axis_index("rep")
    nf = lax.axis_size("fsdp")
    brows, bcols = own.shape
    group = nf // brows
    block = G.shape[0]
    slots, band, _ = rl_v.shape
    half = bcols // 2
    up, dn, opp = lax.rem(q + 1, 4), lax.rem(q + 3, 4), lax.rem(q + 2, 4)
    fi, fk, core = f // group, lax.rem(f, group), lax.rem(f, 2)

    def rcopy(src, dst, ssem, rsem, rep, sends=None, receives=None):
        copy = pltpu.make_async_remote_copy(
            src_ref=src, dst_ref=dst, send_sem=ssem, recv_sem=rsem,
            device_id=(f, rep), device_id_type=MESH,
        )
        return Copy(copy, sends, receives)

    loads = [
        pltpu.make_async_copy(src, dst, load_sem.at[n])
        for n, (src, dst) in enumerate(
            [(g_hbm.at[0], g_v), (rl_hbm, rl_v), (rr_hbm, rr_v)]
        )
    ]

    def shift(o):
        return lax.rem(2 * lax.rem(o, 2) + lax.rem(o // 2, 4) + o // 8, 4)

    my_shift = shift(f)
    site_row = lax.rem(q + 4 - my_shift, 4)
    own_row = site_row == fi

    def along_z(n):
        return (lax.rem(f + 8 * n, nf), q)

    def along_x(n):
        return ((f // 8) * 8 + lax.rem(f + n, 8), q)

    near = [along_z(1), along_z(7), along_x(1), along_x(7)]
    further = [along_z(2), along_z(6), along_x(2), along_x(6)]
    x_line = [along_x(n) for n in range(1, 8)]
    y_line = [(f, up), (f, dn), (f, opp)]

    def greet(sem, devices):
        for device in devices:
            pl.semaphore_signal(sem, inc=1, device_id=device, device_id_type=MESH)

    loads[0].start()
    barrier = pltpu.get_barrier_semaphore()
    greet(barrier, y_line + near)
    for load in loads[1:]:
        load.start()

    def column_of(o, carry):
        col = jnp.int32(0)
        for j in range(bcols):
            col = jnp.where(own[fi, j] == o, jnp.int32(j), col)
        jtbl[o] = col
        return carry

    lax.fori_loop(0, nf, column_of, 0)
    held = []
    for t in range(brows):
        count = jnp.int32(0)
        for j in range(bcols):
            count = count + jnp.where(own[t, j] == f, jnp.int32(1), jnp.int32(0))
        held.append(count)
    before = jnp.int32(0)
    for t in range(brows):
        stbl[t] = jnp.minimum(before, slots - 1)
        before = before + held[t]
    slot_row, slot_valid = [], []
    for s in range(slots):
        row, valid = jnp.int32(0), jnp.int32(0)
        before = jnp.int32(0)
        for t in range(brows):
            hit = jnp.where(before == s, held[t], 0)
            row = row + hit * t
            valid = valid + hit
            before = before + held[t]
        slot_row.append(row)
        slot_valid.append(valid)

    def tall(t, c):
        return lax.rem(t + 2 * c, 4) < 2

    tall_q, tall_up, tall_dn, tall_opp = [tall(t, core) for t in (q, up, dn, opp)]

    def lanes(base, group_of):
        return pl.ds(pl.multiple_of(base + group_of * LANES, LANES), LANES)

    loads[0].wait()

    def pack(j, carry):
        base = j * block
        for t in range(4):
            pk[t, j, 0:TALL, :] = g_v[:, lanes(base, t)]
        for t in range(2):
            pk[t + 2 * core, j, TALL:PIECE, :] = g_v[0:32, lanes(base, 4 + t)]
            pk[t + 2 * (1 - core), j, TALL:64, :] = g_v[32:TALL, lanes(base, 4 + t)]
        return carry

    lax.fori_loop(0, bcols, pack, 0)
    pl.semaphore_wait(barrier, len(y_line) + len(near))

    def sums(n):
        row, count = CHUNKS[n]
        lo, hi, rows = pl.ds(0, half), pl.ds(half, half), pl.ds(row, count)
        if n < 2:
            s_up = s_dn = s_opp = r_up = r_dn = r_q = None
        else:
            s_up, s_dn, s_opp, r_up, r_dn, r_q = tall_up, tall_dn, tall_opp, tall_up, tall_dn, tall_q
        ss, rr = rs_s.at[n], rs_r.at[n]
        return [
            rcopy(pk.at[opp, lo, rows], rs_rel.at[0, :, rows], ss.at[0], rr.at[0], dn, s_opp, r_dn),
            rcopy(pk.at[opp, hi, rows], rs_rel.at[1, :, rows], ss.at[1], rr.at[1], up, s_opp, r_up),
            rcopy(pk.at[up, lo, rows], rs_dir.at[0, :, rows], ss.at[2], rr.at[2], up, s_up, r_q),
            rcopy(pk.at[dn, hi, rows], rs_dir.at[1, :, rows], ss.at[3], rr.at[3], dn, s_dn, r_q),
            rcopy(rs_out.at[0, :, rows], rs_acc.at[0, :, rows], ss.at[4], rr.at[4], dn, s_dn, r_q),
            rcopy(rs_out.at[1, :, rows], rs_acc.at[1, :, rows], ss.at[5], rr.at[5], up, s_up, r_q),
        ]

    rs = [sums(n) for n in range(3)]

    def first_sends(n):
        for copy in rs[n][:4]:
            copy.start()

    def relay_sums(n):
        row, count = CHUNKS[n]
        rows = slice(row, row + count)
        for side, first, target in ((0, 0, dn), (1, half, up)):
            rs[n][side].wait_recv()

            def body(j, carry):
                total = rs_rel[side, j, rows].astype(F32) + pk[target, first + j, rows].astype(F32)
                rs_out[side, j, rows] = total.astype(BF16)
                return carry

            lax.fori_loop(0, half, body, 0)
            rs[n][4 + side].start()

    def full_sums(n):
        row, count = CHUNKS[n]
        rows = slice(row, row + count)
        for side, first in ((0, 0), (1, half)):
            rs[n][2 + side].wait_recv()
            rs[n][4 + side].wait_recv()

            def body(j, carry):
                total = pk[q, first + j, rows].astype(F32) + rs_dir[side, j, rows].astype(F32)
                strip[first + j, rows] = (total + rs_acc[side, j, rows].astype(F32)).astype(BF16)
                return carry

            lax.fori_loop(0, half, body, 0)

    def send_pieces(n):
        row, count = CHUNKS[n]
        rows = pl.ds(row, count)

        def piece_copy(o):
            return pltpu.make_async_remote_copy(
                src_ref=out.at[o, rows], dst_ref=gi.at[q, fk, rows], send_sem=a_s.at[n], recv_sem=a_r.at[n],
                device_id=(o, lax.rem(fi + shift(o), 4)), device_id_type=MESH,
            )

        def send_piece(d, carry):
            o = lax.rem(f + d, nf)
            out[o, row : row + count] = strip[jtbl[o], row : row + count]
            piece_copy(o).start()
            return carry

        def send_all():
            lax.fori_loop(1, nf, send_piece, 0)

            @pl.when(own_row)
            def _():
                gi[q, fk, row : row + count] = strip[jtbl[f], row : row + count]

            @pl.when(jnp.logical_not(own_row))
            def _():
                out[f, row : row + count] = strip[jtbl[f], row : row + count]
                piece_copy(f).start()

        gated(None if n < 2 else tall_q, send_all)

    def await_pieces(sem, n, total, here):
        count = CHUNKS[n][1]

        def some(pieces):
            view = out.at[pl.ds(0, pieces), pl.ds(0, count)]
            pltpu.make_async_copy(view, view, sem.at[n]).wait()

        pl.when(here)(lambda: some(total - 1))
        pl.when(jnp.logical_not(here))(lambda: some(total))

    def await_strip(sem, n):
        gated(None if n < 2 else tall_q, lambda: await_pieces(sem, n, nf, own_row))

    def await_block(sem, n):
        if n < 2:
            await_pieces(sem, n, nf, own_row)
        else:
            await_pieces(sem, n, nf // 2, jnp.logical_and(own_row, tall_q))

    def await_all(copies, own_copy):
        for copy in copies:
            copy.wait_recv()
        own_copy.wait()

    def window(t):
        return pl.ds(pl.multiple_of(LANES * (t + t // 2), LANES), 2 * LANES)

    far_out, far_in = ro.at[opp, :, :, window(q)], ri.at[q, :, :, window(q)]
    roots = [
        rcopy(far_out, far_in, ro_s.at[0], ro_r.at[0], opp),
        rcopy(ro.at[up], ri.at[q], ro_s.at[1], ro_r.at[1], up),
        rcopy(ro.at[dn], ri.at[q], ro_s.at[2], ro_r.at[2], dn),
    ]
    roots_own = pltpu.make_async_copy(ro.at[q], ri.at[q], copy_sem.at[0])

    first_sends(0)
    greet(near_sem, near)
    first_sends(1)
    pl.semaphore_wait(near_sem, len(near))
    greet(line_sem, further)
    loads[1].wait()
    loads[2].wait()
    for t in range(4):
        slot = stbl[lax.rem(t + 4 - my_shift, 4)]
        ro[t, 0] = rl_v[slot]
        ro[t, 1] = rr_v[slot]
    pl.semaphore_wait(line_sem, len(further))
    greet(plane_sem, x_line)
    relay_sums(0)
    first_sends(2)
    pl.semaphore_wait(plane_sem, len(x_line))
    greet(cube_sem, y_line)
    relay_sums(1)
    full_sums(0)
    pl.semaphore_wait(cube_sem, len(y_line))
    send_pieces(0)
    relay_sums(2)
    for copy in roots:
        copy.start()
    roots_own.start()
    full_sums(1)
    send_pieces(1)
    full_sums(2)
    send_pieces(2)
    await_all(roots, roots_own)
    for n in range(2):
        turned[...] = ri[:, n, :, window(opp)].reshape(block, 2 * LANES).T
        ri[opp, n] = turned[pl.ds(pl.multiple_of(64 * lax.rem(opp, 2), 16), band), :]

    for n in range(3):
        await_block(a_r, n)

    def unpack_block(k, carry):
        c = lax.rem(k, 2)
        row0 = pl.multiple_of(k * TALL, 16)
        for t in range(4):
            G[pl.ds(row0, TALL), t * LANES : (t + 1) * LANES] = gi[t, k, 0:TALL, :]
        for t in range(2):
            into = slice((4 + t) * LANES, (5 + t) * LANES)
            G[pl.ds(row0, 32), into] = gi[t + 2 * c, k, TALL:PIECE, :]
            G[pl.ds(pl.multiple_of(row0 + 32, 16), 16), into] = gi[t + 2 * (1 - c), k, TALL:64, :]
        return carry

    lax.fori_loop(0, group, unpack_block, 0)

    def exchange(n):
        ss, rr = t_s.at[n], t_r.at[n]
        return [
            rcopy(to.at[n, opp], ti.at[n, q], ss.at[0], rr.at[0], opp),
            rcopy(to.at[n, up], ti.at[n, q], ss.at[1], rr.at[1], up),
            rcopy(to.at[n, dn], ti.at[n, q], ss.at[2], rr.at[2], dn),
        ], pltpu.make_async_copy(to.at[n, q], ti.at[n, q], copy_sem.at[1 + n])

    def products_left(c, carry):
        rows = G[pl.ds(pl.multiple_of(c * band, 16), band), :]
        to[0, c] = lax.dot_general(
            rows, G[...], (((1,), (1,)), ((), ())), preferred_element_type=F32
        ).astype(BF16)
        return carry

    def products_right(c, carry):
        rows = GT[pl.ds(pl.multiple_of(c * band, 16), band), :]
        to[1, c] = jnp.dot(rows, G[...], preferred_element_type=F32).astype(BF16)
        return carry

    stats = [exchange(n) for n in range(2)]

    def send_products(n):
        copies, own_copy = stats[n]
        for copy in copies:
            copy.start()
        own_copy.start()

    lax.fori_loop(0, 4, products_left, 0)
    send_products(0)
    GT[...] = G[...].T
    lax.fori_loop(0, 4, products_right, 0)
    send_products(1)

    per_band = band // TALL

    def precondition(b, carry):
        p = jnp.dot(ri[b, 0], G[...], preferred_element_type=F32).astype(BF16)
        u = jnp.dot(p, ri[:, 1].reshape(block, block), preferred_element_type=F32).astype(BF16)
        for n in range(per_band):
            k = b * per_band + n
            row0, c = n * TALL, n % 2
            for t in range(4):
                uo[t, k, 0:TALL, :] = u[row0 : row0 + TALL, t * LANES : (t + 1) * LANES]
            for t in range(2):
                part = u[row0 : row0 + TALL, (4 + t) * LANES : (5 + t) * LANES]
                uo[t + 2 * c, k, TALL:PIECE, :] = part[0:32]
                uo[t + 2 * (1 - c), k, TALL:64, :] = part[32:TALL]
        return carry

    lax.fori_loop(0, 4, precondition, 0)

    rb = (rb0, rb1, rb2)

    def send_back(n):
        row, count = CHUNKS[n]
        rows = pl.ds(row, count)

        def one(e, carry):
            if n < 2:
                t, k = lax.rem(e, 4), lax.rem(e // 4 + fk, group)
            else:
                k = lax.rem(e // 2 + fk, group)
                t = 2 * lax.rem(k, 2) + lax.rem(e, 2)
            p = site_row * group + k
            copy = pltpu.make_async_remote_copy(
                src_ref=uo.at[t, k, rows], dst_ref=rb[n].at[f], send_sem=b_s.at[n], recv_sem=b_r.at[n],
                device_id=(p, t), device_id_type=MESH,
            )

            @pl.when(jnp.logical_not(jnp.logical_and(p == f, t == q)))
            def _():
                copy.start()

            return carry

        lax.fori_loop(0, nf if n < 2 else nf // 2, one, 0)

        @pl.when(own_row)
        def _():
            rb[n][f] = uo[q, fk, row : row + count]

    for n in range(3):
        send_back(n)

    def spread(n):
        row, count = CHUNKS[n]
        lo, hi, rows = pl.ds(0, half), pl.ds(half, half), pl.ds(row, count)
        if n < 2:
            t_q = t_up = t_dn = t_opp = None
        else:
            t_q, t_up, t_dn, t_opp = tall_q, tall_up, tall_dn, tall_opp
        ss, rr = ag_s.at[n], ag_r.at[n]
        mine = ag.at[q, :, rows]
        from_up, from_dn = ag.at[up, lo, rows], ag.at[dn, hi, rows]
        return [
            rcopy(mine, mine, ss.at[0], rr.at[0], up, t_q, t_dn),
            rcopy(mine, mine, ss.at[1], rr.at[1], dn, t_q, t_up),
            rcopy(from_up, from_up, ss.at[2], rr.at[2], dn, t_up, t_opp),
            rcopy(from_dn, from_dn, ss.at[3], rr.at[3], up, t_dn, t_opp),
        ]

    gather = [spread(n) for n in range(3)]

    def start_gather(n):
        row, count = CHUNKS[n]
        await_strip(b_r, n)

        def pick(j, carry):
            ag[q, j, row : row + count] = rb[n][own[fi, j]]
            return carry

        lax.fori_loop(0, bcols, pick, 0)
        gather[n][0].start()
        gather[n][1].start()

    def forward_gather(n):
        gather[n][1].wait_recv()
        gather[n][2].start()
        gather[n][0].wait_recv()
        gather[n][3].start()

    start_gather(0)
    start_gather(1)
    forward_gather(0)
    start_gather(2)
    forward_gather(1)
    forward_gather(2)

    for copies, own_copy in stats:
        await_all(copies, own_copy)
    for s in range(slots):
        decay[s] = jnp.where(slot_valid[s] > 0, jnp.float32(stat_decay), jnp.float32(1.0))
        for n in range(2):
            term = ti[n, lax.rem(slot_row[s] + my_shift, 4)]
            terms[n, s] = jnp.where(slot_valid[s] > 0, term, jnp.zeros_like(term))
    stores = [pltpu.make_async_copy(terms, terms_hbm, store_sem.at[0])] + [
        pltpu.make_async_copy(up_v.at[pl.ds(row, 16)], up_hbm.at[pl.ds(row, 16)], store_sem.at[1 + n])
        for n, row in enumerate((0, 32, 16))
    ]
    stores[0].start()

    def finish_gather(n):
        gather[n][2].wait_recv()
        gather[n][3].wait_recv()

        def unpack_row(j, carry):
            base = j * block
            if n == 0:
                for t in range(4):
                    up_v[0:32, lanes(base, t)] = ag[t, j, 0:32, :]
            elif n == 1:
                for t in range(4):
                    up_v[32:TALL, lanes(base, t)] = ag[t, j, 32:TALL, :]
                for t in range(2):
                    up_v[0:16, lanes(base, 4 + t)] = ag[t + 2 * core, j, TALL:64, :]
                    up_v[32:TALL, lanes(base, 4 + t)] = ag[t + 2 * (1 - core), j, TALL:64, :]
            else:
                for t in range(2):
                    up_v[16:32, lanes(base, 4 + t)] = ag[t + 2 * core, j, 64:PIECE, :]
            return carry

        lax.fori_loop(0, bcols, unpack_row, 0)

    finish_gather(0)
    finish_gather(1)
    stores[1].start()
    stores[2].start()
    finish_gather(2)
    stores[3].start()

    for copies in rs + [roots, stats[0][0], stats[1][0]] + gather:
        for copy in copies:
            copy.wait_send()
    for n in range(3):
        await_strip(a_s, n)
        await_block(b_s, n)
    for store in stores:
        store.wait()


def shards(grads, owner_map, stats_left, stats_right, roots_left, roots_right):
    _, rows, width = grads.shape
    slots, band, block = stats_left.shape
    brows, bcols = owner_map.shape
    nf = lax.axis_size("fsdp")
    group = nf // brows
    half = bcols // 2
    dma, count, reg = pltpu.SemaphoreType.DMA, pltpu.SemaphoreType.REGULAR, pltpu.VMEM
    msg = (PIECE, LANES)
    scratch = [
        reg((rows, width), BF16),
        reg((4, bcols) + msg, BF16),
        reg((2, half) + msg, BF16),
        reg((2, half) + msg, BF16),
        reg((2, half) + msg, BF16),
        reg((2, half) + msg, BF16),
        reg((bcols,) + msg, BF16),
        reg((nf,) + msg, BF16),
        reg((4, 2, band, block), BF16),
        reg((4, 2, band, block), BF16),
        reg((2 * LANES, block), BF16),
        reg((4, group) + msg, BF16),
        reg((block, block), BF16),
        reg((block, block), BF16),
        reg((4, group) + msg, BF16),
        reg((nf, 32, LANES), BF16),
        reg((nf, 32, LANES), BF16),
        reg((nf, 16, LANES), BF16),
        reg((4, bcols) + msg, BF16),
        reg((2, 4, band, block), BF16),
        reg((2, 4, band, block), BF16),
        reg((2, slots, band, block), BF16),
        reg((slots, band, block), BF16),
        reg((slots, band, block), BF16),
        reg((rows, width), BF16),
        pltpu.SMEM((nf,), jnp.int32),
        pltpu.SMEM((brows,), jnp.int32),
        dma((3,)), dma((3,)), dma((4,)), count, count, count, count,
        dma((3, 6)), dma((3, 6)), dma((3,)), dma((3,)), dma((3,)), dma((3,)),
        dma((3,)), dma((3,)), dma((2, 3)), dma((2, 3)), dma((3, 4)), dma((3, 4)),
    ]
    hbm = pl.BlockSpec(memory_space=pl.ANY)
    decay, terms, update = pl.pallas_call(
        kernel,
        out_shape=(
            jax.ShapeDtypeStruct((slots,), F32),
            jax.ShapeDtypeStruct((2, slots, band, block), BF16),
            jax.ShapeDtypeStruct((rows, width), BF16),
        ),
        in_specs=[pl.BlockSpec(memory_space=pltpu.SMEM)] + [hbm] * 3,
        out_specs=(pl.BlockSpec(memory_space=pltpu.SMEM), hbm, hbm),
        scratch_shapes=scratch,
        compiler_params=pltpu.CompilerParams(
            collective_id=0, has_side_effects=True, vmem_limit_bytes=60 * 1024 * 1024
        ),
        name="shampoo",
    )(owner_map, grads, roots_left, roots_right)
    keep = decay[:, None, None]
    new_left = keep * stats_left + (1.0 - stat_decay) * terms[0].astype(F32)
    new_right = keep * stats_right + (1.0 - stat_decay) * terms[1].astype(F32)
    return new_left, new_right, update


def solution(mesh):
    in_specs = (
        P("rep", "fsdp", None),
        P(),
        P("fsdp", "rep", None),
        P("fsdp", "rep", None),
        P("fsdp", "rep", None),
        P("fsdp", "rep", None),
    )
    out_specs = (P("fsdp", "rep", None), P("fsdp", "rep", None), P("fsdp", None))
    return jax.shard_map(shards, mesh=mesh, in_specs=in_specs, out_specs=out_specs, check_vma=False)
```

```python
import jax
import jax.numpy as jnp
from jax import lax
from jax.experimental import pallas as pl
from jax.experimental.pallas import tpu as pltpu
from jax.sharding import PartitionSpec as P

stat_decay = 0.95
MESH = pl.DeviceIdType.MESH
LANES = 128
TALL = 48
PIECE = 80
CHUNKS = ((0, 32), (32, 32), (64, 16))
LAST = len(CHUNKS) - 1
BF16 = jnp.bfloat16
F32 = jnp.float32


class Copy:
    def __init__(self, copy, sends=None, receives=None):
        self.copy, self.sends, self.receives = copy, sends, receives

    def start(self):
        gated(self.sends, self.copy.start)

    def wait_send(self):
        gated(self.sends, self.copy.wait_send)

    def wait_recv(self):
        gated(self.receives, self.copy.wait_recv)


def gated(condition, act):
    if condition is None:
        act()
    else:

        @pl.when(condition)
        def _():
            act()


def kernel(
    own, g_hbm, rl_hbm, rr_hbm,
    decay, terms_hbm, up_hbm,
    g_v, pk, rs_rel, rs_dir, rs_acc, rs_out, strip,
    out, ro, ri, turned, gi, G, GT,
    uo, rb0, rb1, rb2, ag, to, ti, terms,
    rl_v, rr_v, up_v, jtbl, stbl,
    load_sem, copy_sem, store_sem, near_sem, line_sem, plane_sem, cube_sem,
    rs_s, rs_r, a_s, a_r, ro_s, ro_r, b_s, b_r, t_s, t_r, ag_s, ag_r,
):
    f = lax.axis_index("fsdp")
    q = lax.axis_index("rep")
    nf = lax.axis_size("fsdp")
    brows, bcols = own.shape
    group = nf // brows
    block = G.shape[0]
    slots, band, _ = rl_v.shape
    half = bcols // 2
    up, dn, opp = lax.rem(q + 1, 4), lax.rem(q + 3, 4), lax.rem(q + 2, 4)
    fi, fk, core = f // group, lax.rem(f, group), lax.rem(f, 2)

    def rcopy(src, dst, ssem, rsem, rep, sends=None, receives=None):
        copy = pltpu.make_async_remote_copy(
            src_ref=src, dst_ref=dst, send_sem=ssem, recv_sem=rsem,
            device_id=(f, rep), device_id_type=MESH,
        )
        return Copy(copy, sends, receives)

    loads = [
        pltpu.make_async_copy(src, dst, load_sem.at[n])
        for n, (src, dst) in enumerate(
            [(g_hbm.at[0], g_v), (rl_hbm, rl_v), (rr_hbm, rr_v)]
        )
    ]

    def shift(o):
        return lax.rem(2 * lax.rem(o, 2) + lax.rem(o // 2, 4) + o // 8, 4)

    my_shift = shift(f)
    site_row = lax.rem(q + 4 - my_shift, 4)
    own_row = site_row == fi

    def along_z(n):
        return (lax.rem(f + 8 * n, nf), q)

    def along_x(n):
        return ((f // 8) * 8 + lax.rem(f + n, 8), q)

    near = [along_z(1), along_z(7), along_x(1), along_x(7)]
    further = [along_z(2), along_z(6), along_x(2), along_x(6)]
    x_line = [along_x(n) for n in range(1, 8)]
    y_line = [(f, up), (f, dn), (f, opp)]

    def greet(sem, devices):
        for device in devices:
            pl.semaphore_signal(sem, inc=1, device_id=device, device_id_type=MESH)

    loads[0].start()
    barrier = pltpu.get_barrier_semaphore()
    greet(barrier, y_line + near)
    for load in loads[1:]:
        load.start()

    def column_of(o, carry):
        col = jnp.int32(0)
        for j in range(bcols):
            col = jnp.where(own[fi, j] == o, jnp.int32(j), col)
        jtbl[o] = col
        return carry

    lax.fori_loop(0, nf, column_of, 0)
    held = []
    for t in range(brows):
        count = jnp.int32(0)
        for j in range(bcols):
            count = count + jnp.where(own[t, j] == f, jnp.int32(1), jnp.int32(0))
        held.append(count)
    before = jnp.int32(0)
    for t in range(brows):
        stbl[t] = jnp.minimum(before, slots - 1)
        before = before + held[t]
    slot_row, slot_valid = [], []
    for s in range(slots):
        row, valid = jnp.int32(0), jnp.int32(0)
        before = jnp.int32(0)
        for t in range(brows):
            hit = jnp.where(before == s, held[t], 0)
            row = row + hit * t
            valid = valid + hit
            before = before + held[t]
        slot_row.append(row)
        slot_valid.append(valid)

    def tall(t, c):
        return lax.rem(t + 2 * c, 4) < 2

    tall_q, tall_up, tall_dn, tall_opp = [tall(t, core) for t in (q, up, dn, opp)]

    def lanes(base, group_of):
        return pl.ds(pl.multiple_of(base + group_of * LANES, LANES), LANES)

    loads[0].wait()

    def pack(j, carry):
        base = j * block
        for t in range(4):
            pk[t, j, 0:TALL, :] = g_v[:, lanes(base, t)]
        for t in range(2):
            pk[t + 2 * core, j, TALL:PIECE, :] = g_v[0:32, lanes(base, 4 + t)]
            pk[t + 2 * (1 - core), j, TALL:64, :] = g_v[32:TALL, lanes(base, 4 + t)]
        return carry

    lax.fori_loop(0, bcols, pack, 0)
    pl.semaphore_wait(barrier, len(y_line) + len(near))

    def sums(n):
        row, count = CHUNKS[n]
        lo, hi, rows = pl.ds(0, half), pl.ds(half, half), pl.ds(row, count)
        if n < LAST:
            s_up = s_dn = s_opp = r_up = r_dn = r_q = None
        else:
            s_up, s_dn, s_opp, r_up, r_dn, r_q = tall_up, tall_dn, tall_opp, tall_up, tall_dn, tall_q
        ss, rr = rs_s.at[n], rs_r.at[n]
        return [
            rcopy(pk.at[opp, lo, rows], rs_rel.at[0, :, rows], ss.at[0], rr.at[0], dn, s_opp, r_dn),
            rcopy(pk.at[opp, hi, rows], rs_rel.at[1, :, rows], ss.at[1], rr.at[1], up, s_opp, r_up),
            rcopy(pk.at[up, lo, rows], rs_dir.at[0, :, rows], ss.at[2], rr.at[2], up, s_up, r_q),
            rcopy(pk.at[dn, hi, rows], rs_dir.at[1, :, rows], ss.at[3], rr.at[3], dn, s_dn, r_q),
            rcopy(rs_out.at[0, :, rows], rs_acc.at[0, :, rows], ss.at[4], rr.at[4], dn, s_dn, r_q),
            rcopy(rs_out.at[1, :, rows], rs_acc.at[1, :, rows], ss.at[5], rr.at[5], up, s_up, r_q),
        ]

    rs = [sums(n) for n in range(len(CHUNKS))]

    def first_sends(n):
        for copy in rs[n][:4]:
            copy.start()

    def relay_sums(n):
        row, count = CHUNKS[n]
        rows = slice(row, row + count)
        for side, first, target in ((0, 0, dn), (1, half, up)):
            rs[n][side].wait_recv()

            def body(j, carry):
                total = rs_rel[side, j, rows].astype(F32) + pk[target, first + j, rows].astype(F32)
                rs_out[side, j, rows] = total.astype(BF16)
                return carry

            lax.fori_loop(0, half, body, 0)
            rs[n][4 + side].start()

    def full_sums(n):
        row, count = CHUNKS[n]
        rows = slice(row, row + count)
        for side, first in ((0, 0), (1, half)):
            rs[n][2 + side].wait_recv()
            rs[n][4 + side].wait_recv()

            def body(j, carry):
                total = pk[q, first + j, rows].astype(F32) + rs_dir[side, j, rows].astype(F32)
                strip[first + j, rows] = (total + rs_acc[side, j, rows].astype(F32)).astype(BF16)
                return carry

            lax.fori_loop(0, half, body, 0)

    def send_pieces(n):
        row, count = CHUNKS[n]
        rows = pl.ds(row, count)

        def piece_copy(o):
            return pltpu.make_async_remote_copy(
                src_ref=out.at[o, rows], dst_ref=gi.at[q, fk, rows], send_sem=a_s.at[n], recv_sem=a_r.at[n],
                device_id=(o, lax.rem(fi + shift(o), 4)), device_id_type=MESH,
            )

        def send_piece(d, carry):
            o = lax.rem(f + d, nf)
            out[o, row : row + count] = strip[jtbl[o], row : row + count]
            piece_copy(o).start()
            return carry

        def send_all():
            lax.fori_loop(1, nf, send_piece, 0)

            @pl.when(own_row)
            def _():
                gi[q, fk, row : row + count] = strip[jtbl[f], row : row + count]

            @pl.when(jnp.logical_not(own_row))
            def _():
                out[f, row : row + count] = strip[jtbl[f], row : row + count]
                piece_copy(f).start()

        gated(None if n < LAST else tall_q, send_all)

    def await_pieces(sem, n, total, here):
        count = CHUNKS[n][1]

        def some(pieces):
            view = out.at[pl.ds(0, pieces), pl.ds(0, count)]
            pltpu.make_async_copy(view, view, sem.at[n]).wait()

        pl.when(here)(lambda: some(total - 1))
        pl.when(jnp.logical_not(here))(lambda: some(total))

    def await_strip(sem, n):
        gated(None if n < LAST else tall_q, lambda: await_pieces(sem, n, nf, own_row))

    def await_block(sem, n):
        if n < LAST:
            await_pieces(sem, n, nf, own_row)
        else:
            await_pieces(sem, n, nf // 2, jnp.logical_and(own_row, tall_q))

    def await_all(copies, own_copy):
        for copy in copies:
            copy.wait_recv()
        own_copy.wait()

    def window(t):
        return pl.ds(pl.multiple_of(LANES * (t + t // 2), LANES), 2 * LANES)

    def inner(t):
        return (3 * t + 1) // 2

    def inner_rows(t):
        return pl.ds(pl.multiple_of(64 * lax.rem(t, 2), 16), LANES)

    def differs(m, t, u):
        return jnp.logical_and(inner(t) != m, inner(u) != m)

    far_out, far_in = ro.at[opp, :, :, window(q)], ri.at[q, :, :, window(q)]
    roots = [rcopy(far_out, far_in, ro_s.at[0], ro_r.at[0], opp)]
    for n, (to_rep, from_rep) in enumerate(((dn, up), (up, dn))):
        more = lanes(0, inner(opp))
        k = 1 + 7 * n
        roots.append(rcopy(ro.at[to_rep, n, :, more], ri.at[q, n, :, more], ro_s.at[k], ro_r.at[k], to_rep))
        for m in range(block // LANES):
            cols = pl.ds(m * LANES, LANES)
            k = 2 + 7 * n + m
            roots.append(
                rcopy(
                    ro.at[to_rep, :, :, cols], ri.at[q, :, :, cols], ro_s.at[k], ro_r.at[k], to_rep,
                    differs(m, to_rep, opp), differs(m, q, to_rep),
                )
            )
    roots_own = pltpu.make_async_copy(ro.at[q], ri.at[q], copy_sem.at[0])

    def start_roots():
        for copy in roots:
            copy.start()
        roots_own.start()

    first_sends(0)
    greet(near_sem, near)
    first_sends(1)
    pl.semaphore_wait(near_sem, len(near))
    greet(line_sem, further)
    loads[1].wait()
    loads[2].wait()
    for t in range(4):
        slot = stbl[lax.rem(t + 4 - my_shift, 4)]
        ro[t, 0] = rl_v[slot]
        ro[t, 1] = rr_v[slot]
    pl.semaphore_wait(line_sem, len(further))
    greet(plane_sem, x_line)
    for n in range(LAST + 1):
        relay_sums(n)
        if n + 2 <= LAST:
            first_sends(n + 2)
        if n == 0:
            pl.semaphore_wait(plane_sem, len(x_line))
            greet(cube_sem, y_line)
        if n == LAST:
            start_roots()
        if n >= 1:
            full_sums(n - 1)
            if n == 1:
                pl.semaphore_wait(cube_sem, len(y_line))
            send_pieces(n - 1)
    full_sums(LAST)
    send_pieces(LAST)
    await_all(roots, roots_own)
    for n, (x, y) in enumerate(((up, dn), (dn, up))):
        mine = lanes(0, inner(q))
        ri[:, n, :, mine] = ri[q, n, inner_rows(q), :].T.reshape(4, band, LANES)
        turned[:, 0:LANES] = ri[x, n, inner_rows(x), window(y)].T
        ri[y, n, :, lanes(0, inner(x))] = turned[pl.ds(pl.multiple_of(64 * lax.rem(y, 2), 16), band), 0:LANES]
        turned[...] = ri[:, n, :, window(opp)].reshape(block, 2 * LANES).T
        ri[opp, n] = turned[pl.ds(pl.multiple_of(64 * lax.rem(opp, 2), 16), band), :]

    for n in range(len(CHUNKS)):
        await_block(a_r, n)

    def unpack_block(k, carry):
        c = lax.rem(k, 2)
        row0 = pl.multiple_of(k * TALL, 16)
        for t in range(4):
            G[pl.ds(row0, TALL), t * LANES : (t + 1) * LANES] = gi[t, k, 0:TALL, :]
        for t in range(2):
            into = slice((4 + t) * LANES, (5 + t) * LANES)
            G[pl.ds(row0, 32), into] = gi[t + 2 * c, k, TALL:PIECE, :]
            G[pl.ds(pl.multiple_of(row0 + 32, 16), 16), into] = gi[t + 2 * (1 - c), k, TALL:64, :]
        return carry

    lax.fori_loop(0, group, unpack_block, 0)

    def exchange(n):
        ss, rr = t_s.at[n], t_r.at[n]
        return [
            rcopy(to.at[n, opp], ti.at[n, q], ss.at[0], rr.at[0], opp),
            rcopy(to.at[n, up], ti.at[n, q], ss.at[1], rr.at[1], up),
            rcopy(to.at[n, dn], ti.at[n, q], ss.at[2], rr.at[2], dn),
        ], pltpu.make_async_copy(to.at[n, q], ti.at[n, q], copy_sem.at[1 + n])

    def products_left(c, carry):
        rows = G[pl.ds(pl.multiple_of(c * band, 16), band), :]
        to[0, c] = lax.dot_general(
            rows, G[...], (((1,), (1,)), ((), ())), preferred_element_type=F32
        ).astype(BF16)
        return carry

    def products_right(c, carry):
        rows = GT[pl.ds(pl.multiple_of(c * band, 16), band), :]
        to[1, c] = jnp.dot(rows, G[...], preferred_element_type=F32).astype(BF16)
        return carry

    stats = [exchange(n) for n in range(2)]

    def send_products(n):
        copies, own_copy = stats[n]
        for copy in copies:
            copy.start()
        own_copy.start()

    lax.fori_loop(0, 4, products_left, 0)
    send_products(0)
    per_band = band // TALL

    def precondition(b, carry):
        p = jnp.dot(ri[b, 0], G[...], preferred_element_type=F32).astype(BF16)
        u = jnp.dot(p, ri[:, 1].reshape(block, block), preferred_element_type=F32).astype(BF16)
        for n in range(per_band):
            k = b * per_band + n
            row0, c = n * TALL, n % 2
            for t in range(4):
                uo[t, k, 0:TALL, :] = u[row0 : row0 + TALL, t * LANES : (t + 1) * LANES]
            for t in range(2):
                part = u[row0 : row0 + TALL, (4 + t) * LANES : (5 + t) * LANES]
                uo[t + 2 * c, k, TALL:PIECE, :] = part[0:32]
                uo[t + 2 * (1 - c), k, TALL:64, :] = part[32:TALL]
        return carry

    lax.fori_loop(0, 4, precondition, 0)

    rb = (rb0, rb1, rb2)

    def send_back(n):
        row, count = CHUNKS[n]
        rows = pl.ds(row, count)

        def one(e, carry):
            if n < LAST:
                t, k = lax.rem(e, 4), lax.rem(e // 4 + fk, group)
            else:
                k = lax.rem(e // 2 + fk, group)
                t = 2 * lax.rem(k, 2) + lax.rem(e, 2)
            p = site_row * group + k
            copy = pltpu.make_async_remote_copy(
                src_ref=uo.at[t, k, rows], dst_ref=rb[n].at[f], send_sem=b_s.at[n], recv_sem=b_r.at[n],
                device_id=(p, t), device_id_type=MESH,
            )

            @pl.when(jnp.logical_not(jnp.logical_and(p == f, t == q)))
            def _():
                copy.start()

            return carry

        lax.fori_loop(0, nf if n < LAST else nf // 2, one, 0)

        @pl.when(own_row)
        def _():
            rb[n][f] = uo[q, fk, row : row + count]

    for n in range(len(CHUNKS)):
        send_back(n)

    GT[...] = G[...].T
    lax.fori_loop(0, 4, products_right, 0)

    send_products(1)
    def spread(n):
        row, count = CHUNKS[n]
        lo, hi, rows = pl.ds(0, half), pl.ds(half, half), pl.ds(row, count)
        if n < LAST:
            t_q = t_up = t_dn = t_opp = None
        else:
            t_q, t_up, t_dn, t_opp = tall_q, tall_up, tall_dn, tall_opp
        ss, rr = ag_s.at[n], ag_r.at[n]
        mine = ag.at[q, :, rows]
        from_up, from_dn = ag.at[up, lo, rows], ag.at[dn, hi, rows]
        return [
            rcopy(mine, mine, ss.at[0], rr.at[0], up, t_q, t_dn),
            rcopy(mine, mine, ss.at[1], rr.at[1], dn, t_q, t_up),
            rcopy(from_up, from_up, ss.at[2], rr.at[2], dn, t_up, t_opp),
            rcopy(from_dn, from_dn, ss.at[3], rr.at[3], up, t_dn, t_opp),
        ]

    gather = [spread(n) for n in range(len(CHUNKS))]

    def start_gather(n):
        row, count = CHUNKS[n]
        await_strip(b_r, n)

        def pick(j, carry):
            ag[q, j, row : row + count] = rb[n][own[fi, j]]
            return carry

        lax.fori_loop(0, bcols, pick, 0)
        gather[n][0].start()
        gather[n][1].start()

    def forward_gather(n):
        gather[n][1].wait_recv()
        gather[n][2].start()
        gather[n][0].wait_recv()
        gather[n][3].start()

    for n in range(LAST + 1):
        start_gather(n)
        if n >= 1:
            forward_gather(n - 1)
    forward_gather(LAST)

    for copies, own_copy in stats:
        await_all(copies, own_copy)
    for s in range(slots):
        decay[s] = jnp.where(slot_valid[s] > 0, jnp.float32(stat_decay), jnp.float32(1.0))
        for n in range(2):
            term = ti[n, lax.rem(slot_row[s] + my_shift, 4)]
            terms[n, s] = jnp.where(slot_valid[s] > 0, term, jnp.zeros_like(term))
    stores = [pltpu.make_async_copy(terms, terms_hbm, store_sem.at[0])] + [
        pltpu.make_async_copy(up_v.at[pl.ds(row, 16)], up_hbm.at[pl.ds(row, 16)], store_sem.at[1 + n])
        for n, row in enumerate((0, 32, 16))
    ]
    stores[0].start()

    def finish_gather(n):
        gather[n][2].wait_recv()
        gather[n][3].wait_recv()

        row, count = CHUNKS[n]
        end = row + count

        def unpack_row(j, carry):
            base = j * block
            if row < TALL:
                rows = slice(row, min(end, TALL))
                for t in range(4):
                    up_v[rows, lanes(base, t)] = ag[t, j, rows, :]
            for t in range(2):
                if row < 64 and end > TALL:
                    up_v[0:16, lanes(base, 4 + t)] = ag[t + 2 * core, j, TALL:64, :]
                    up_v[32:TALL, lanes(base, 4 + t)] = ag[t + 2 * (1 - core), j, TALL:64, :]
                if n == LAST:
                    up_v[16:32, lanes(base, 4 + t)] = ag[t + 2 * core, j, 64:PIECE, :]
            return carry

        lax.fori_loop(0, bcols, unpack_row, 0)

    for n in range(LAST):
        finish_gather(n)
    stores[1].start()
    stores[2].start()
    finish_gather(LAST)
    stores[3].start()

    for copies in rs + [roots, stats[0][0], stats[1][0]] + gather:
        for copy in copies:
            copy.wait_send()
    for n in range(len(CHUNKS)):
        await_strip(a_s, n)
        await_block(b_s, n)
    for store in stores:
        store.wait()


def shards(grads, owner_map, stats_left, stats_right, roots_left, roots_right):
    _, rows, width = grads.shape
    slots, band, block = stats_left.shape
    brows, bcols = owner_map.shape
    nf = lax.axis_size("fsdp")
    group = nf // brows
    half = bcols // 2
    parts = len(CHUNKS)
    dma, tally, reg = pltpu.SemaphoreType.DMA, pltpu.SemaphoreType.REGULAR, pltpu.VMEM
    msg = (PIECE, LANES)
    scratch = [
        reg((rows, width), BF16),
        reg((4, bcols) + msg, BF16),
        reg((2, half) + msg, BF16),
        reg((2, half) + msg, BF16),
        reg((2, half) + msg, BF16),
        reg((2, half) + msg, BF16),
        reg((bcols,) + msg, BF16),
        reg((nf,) + msg, BF16),
        reg((4, 2, band, block), BF16),
        reg((4, 2, band, block), BF16),
        reg((2 * LANES, block), BF16),
        reg((4, group) + msg, BF16),
        reg((block, block), BF16),
        reg((block, block), BF16),
        reg((4, group) + msg, BF16),
        *[reg((nf, count, LANES), BF16) for _, count in CHUNKS],
        reg((4, bcols) + msg, BF16),
        reg((2, 4, band, block), BF16),
        reg((2, 4, band, block), BF16),
        reg((2, slots, band, block), BF16),
        reg((slots, band, block), BF16),
        reg((slots, band, block), BF16),
        reg((rows, width), BF16),
        pltpu.SMEM((nf,), jnp.int32),
        pltpu.SMEM((brows,), jnp.int32),
        dma((3,)), dma((3,)), dma((4,)), tally, tally, tally, tally,
        dma((parts, 6)), dma((parts, 6)), dma((parts,)), dma((parts,)), dma((15,)), dma((15,)),
        dma((parts,)), dma((parts,)), dma((2, 3)), dma((2, 3)), dma((parts, 4)), dma((parts, 4)),
    ]
    hbm = pl.BlockSpec(memory_space=pl.ANY)
    decay, terms, update = pl.pallas_call(
        kernel,
        out_shape=(
            jax.ShapeDtypeStruct((slots,), F32),
            jax.ShapeDtypeStruct((2, slots, band, block), BF16),
            jax.ShapeDtypeStruct((rows, width), BF16),
        ),
        in_specs=[pl.BlockSpec(memory_space=pltpu.SMEM)] + [hbm] * 3,
        out_specs=(pl.BlockSpec(memory_space=pltpu.SMEM), hbm, hbm),
        scratch_shapes=scratch,
        compiler_params=pltpu.CompilerParams(
            collective_id=0, has_side_effects=True, vmem_limit_bytes=60 * 1024 * 1024
        ),
        name="shampoo",
    )(owner_map, grads, roots_left, roots_right)
    keep = decay[:, None, None]
    new_left = keep * stats_left + (1.0 - stat_decay) * terms[0].astype(F32)
    new_right = keep * stats_right + (1.0 - stat_decay) * terms[1].astype(F32)
    return new_left, new_right, update


def solution(mesh):
    in_specs = (
        P("rep", "fsdp", None),
        P(),
        P("fsdp", "rep", None),
        P("fsdp", "rep", None),
        P("fsdp", "rep", None),
        P("fsdp", "rep", None),
    )
    out_specs = (P("fsdp", "rep", None), P("fsdp", "rep", None), P("fsdp", None))
    return jax.shard_map(shards, mesh=mesh, in_specs=in_specs, out_specs=out_specs, check_vma=False)
```

```python
import jax
import jax.numpy as jnp
from jax import lax
from jax.experimental import pallas as pl
from jax.experimental.pallas import tpu as pltpu
from jax.sharding import PartitionSpec as P

stat_decay = 0.95
MESH = pl.DeviceIdType.MESH
LANES = 128
TALL = 48
PIECE = 80
CHUNKS = ((0, 32), (32, 32), (64, 16))
LAST = len(CHUNKS) - 1
BF16 = jnp.bfloat16
F32 = jnp.float32


class Copy:
    def __init__(self, copy, sends=None, receives=None):
        self.copy, self.sends, self.receives = copy, sends, receives

    def start(self):
        gated(self.sends, self.copy.start)

    def wait_send(self):
        gated(self.sends, self.copy.wait_send)

    def wait_recv(self):
        gated(self.receives, self.copy.wait_recv)


def gated(condition, act):
    if condition is None:
        act()
    else:

        @pl.when(condition)
        def _():
            act()


def kernel(
    own, g_hbm, rl_hbm, rr_hbm,
    decay, terms_hbm, up_hbm,
    g_v, pk, rs_rel, rs_dir, rs_acc, rs_out, strip,
    out, ro, ri, turned, gi, G, GT,
    uo, rb0, rb1, rb2, ag, to, ti, terms,
    rl_v, rr_v, up_v, jtbl, stbl,
    load_sem, copy_sem, store_sem, near_sem, line_sem, plane_sem, cube_sem,
    rs_s, rs_r, a_s, a_r, ro_s, ro_r, b_s, b_r, t_s, t_r, ag_s, ag_r,
):
    f = lax.axis_index("fsdp")
    q = lax.axis_index("rep")
    nf = lax.axis_size("fsdp")
    brows, bcols = own.shape
    group = nf // brows
    block = G.shape[0]
    slots, band, _ = rl_v.shape
    half = bcols // 2
    up, dn, opp = lax.rem(q + 1, 4), lax.rem(q + 3, 4), lax.rem(q + 2, 4)
    fi, fk, core = f // group, lax.rem(f, group), lax.rem(f, 2)

    def rcopy(src, dst, ssem, rsem, rep, sends=None, receives=None):
        copy = pltpu.make_async_remote_copy(
            src_ref=src, dst_ref=dst, send_sem=ssem, recv_sem=rsem,
            device_id=(f, rep), device_id_type=MESH,
        )
        return Copy(copy, sends, receives)

    loads = [
        pltpu.make_async_copy(src, dst, load_sem.at[n])
        for n, (src, dst) in enumerate(
            [(g_hbm.at[0], g_v), (rl_hbm, rl_v), (rr_hbm, rr_v)]
        )
    ]

    def shift(o):
        return lax.rem(2 * lax.rem(o, 2) + lax.rem(o // 2, 4) + o // 8, 4)

    my_shift = shift(f)
    site_row = lax.rem(q + 4 - my_shift, 4)
    own_row = site_row == fi

    def along_z(n):
        return (lax.rem(f + 8 * n, nf), q)

    def along_x(n):
        return ((f // 8) * 8 + lax.rem(f + n, 8), q)

    near = [along_z(1), along_z(7), along_x(1), along_x(7)]
    further = [along_z(2), along_z(6), along_x(2), along_x(6)]
    x_line = [along_x(n) for n in range(1, 8)]
    y_line = [(f, up), (f, dn), (f, opp)]

    def greet(sem, devices):
        for device in devices:
            pl.semaphore_signal(sem, inc=1, device_id=device, device_id_type=MESH)

    loads[0].start()
    barrier = pltpu.get_barrier_semaphore()
    greet(barrier, y_line + near)
    for load in loads[1:]:
        load.start()

    def column_of(o, carry):
        col = jnp.int32(0)
        for j in range(bcols):
            col = jnp.where(own[fi, j] == o, jnp.int32(j), col)
        jtbl[o] = col
        return carry

    lax.fori_loop(0, nf, column_of, 0)
    held = []
    for t in range(brows):
        count = jnp.int32(0)
        for j in range(bcols):
            count = count + jnp.where(own[t, j] == f, jnp.int32(1), jnp.int32(0))
        held.append(count)
    before = jnp.int32(0)
    for t in range(brows):
        stbl[t] = jnp.minimum(before, slots - 1)
        before = before + held[t]
    slot_row, slot_valid = [], []
    for s in range(slots):
        row, valid = jnp.int32(0), jnp.int32(0)
        before = jnp.int32(0)
        for t in range(brows):
            hit = jnp.where(before == s, held[t], 0)
            row = row + hit * t
            valid = valid + hit
            before = before + held[t]
        slot_row.append(row)
        slot_valid.append(valid)

    def tall(t, c):
        return lax.rem(t + 2 * c, 4) < 2

    tall_q, tall_up, tall_dn, tall_opp = [tall(t, core) for t in (q, up, dn, opp)]

    def lanes(base, group_of):
        return pl.ds(pl.multiple_of(base + group_of * LANES, LANES), LANES)

    loads[0].wait()

    def pack(j, carry):
        base = j * block
        for t in range(4):
            pk[t, j, 0:TALL, :] = g_v[:, lanes(base, t)]
        for t in range(2):
            pk[t + 2 * core, j, TALL:PIECE, :] = g_v[0:32, lanes(base, 4 + t)]
            pk[t + 2 * (1 - core), j, TALL:64, :] = g_v[32:TALL, lanes(base, 4 + t)]
        return carry

    lax.fori_loop(0, bcols, pack, 0)
    pl.semaphore_wait(barrier, len(y_line) + len(near))

    def sums(n):
        row, count = CHUNKS[n]
        lo, hi, rows = pl.ds(0, half), pl.ds(half, half), pl.ds(row, count)
        if n < LAST:
            s_up = s_dn = s_opp = r_up = r_dn = r_q = None
        else:
            s_up, s_dn, s_opp, r_up, r_dn, r_q = tall_up, tall_dn, tall_opp, tall_up, tall_dn, tall_q
        ss, rr = rs_s.at[n], rs_r.at[n]
        return [
            rcopy(pk.at[opp, lo, rows], rs_rel.at[0, :, rows], ss.at[0], rr.at[0], dn, s_opp, r_dn),
            rcopy(pk.at[opp, hi, rows], rs_rel.at[1, :, rows], ss.at[1], rr.at[1], up, s_opp, r_up),
            rcopy(pk.at[up, lo, rows], rs_dir.at[0, :, rows], ss.at[2], rr.at[2], up, s_up, r_q),
            rcopy(pk.at[dn, hi, rows], rs_dir.at[1, :, rows], ss.at[3], rr.at[3], dn, s_dn, r_q),
            rcopy(rs_out.at[0, :, rows], rs_acc.at[0, :, rows], ss.at[4], rr.at[4], dn, s_dn, r_q),
            rcopy(rs_out.at[1, :, rows], rs_acc.at[1, :, rows], ss.at[5], rr.at[5], up, s_up, r_q),
        ]

    rs = [sums(n) for n in range(len(CHUNKS))]

    def first_sends(n):
        for copy in rs[n][:4]:
            copy.start()

    def relay_sums(n):
        row, count = CHUNKS[n]
        rows = slice(row, row + count)
        for side, first, target in ((0, 0, dn), (1, half, up)):
            rs[n][side].wait_recv()

            def body(j, carry):
                total = rs_rel[side, j, rows].astype(F32) + pk[target, first + j, rows].astype(F32)
                rs_out[side, j, rows] = total.astype(BF16)
                return carry

            lax.fori_loop(0, half, body, 0)
            rs[n][4 + side].start()

    def full_sums(n):
        row, count = CHUNKS[n]
        rows = slice(row, row + count)
        for side, first in ((0, 0), (1, half)):
            rs[n][2 + side].wait_recv()
            rs[n][4 + side].wait_recv()

            def body(j, carry):
                total = pk[q, first + j, rows].astype(F32) + rs_dir[side, j, rows].astype(F32)
                strip[first + j, rows] = (total + rs_acc[side, j, rows].astype(F32)).astype(BF16)
                return carry

            lax.fori_loop(0, half, body, 0)

    def send_pieces(n):
        row, count = CHUNKS[n]
        rows = pl.ds(row, count)

        def piece_copy(o):
            return pltpu.make_async_remote_copy(
                src_ref=out.at[o, rows], dst_ref=gi.at[q, fk, rows], send_sem=a_s.at[n], recv_sem=a_r.at[n],
                device_id=(o, lax.rem(fi + shift(o), 4)), device_id_type=MESH,
            )

        def send_piece(d, carry):
            o = lax.rem(f + d, nf)
            out[o, row : row + count] = strip[jtbl[o], row : row + count]
            piece_copy(o).start()
            return carry

        def send_all():
            lax.fori_loop(1, nf, send_piece, 0)

            @pl.when(own_row)
            def _():
                gi[q, fk, row : row + count] = strip[jtbl[f], row : row + count]

            @pl.when(jnp.logical_not(own_row))
            def _():
                out[f, row : row + count] = strip[jtbl[f], row : row + count]
                piece_copy(f).start()

        gated(None if n < LAST else tall_q, send_all)

    def await_pieces(sem, n, total, here):
        count = CHUNKS[n][1]

        def some(pieces):
            view = out.at[pl.ds(0, pieces), pl.ds(0, count)]
            pltpu.make_async_copy(view, view, sem.at[n]).wait()

        pl.when(here)(lambda: some(total - 1))
        pl.when(jnp.logical_not(here))(lambda: some(total))

    def await_strip(sem, n):
        gated(None if n < LAST else tall_q, lambda: await_pieces(sem, n, nf, own_row))

    def await_block(sem, n):
        if n < LAST:
            await_pieces(sem, n, nf, own_row)
        else:
            await_pieces(sem, n, nf // 2, jnp.logical_and(own_row, tall_q))

    def await_all(copies, own_copy):
        for copy in copies:
            copy.wait_recv()
        own_copy.wait()

    def window(t):
        return pl.ds(pl.multiple_of(LANES * (t + t // 2), LANES), 2 * LANES)

    def inner(t):
        return (3 * t + 1) // 2

    def inner_rows(t):
        return pl.ds(pl.multiple_of(64 * lax.rem(t, 2), 16), LANES)

    def differs(m, t, u):
        return jnp.logical_and(inner(t) != m, inner(u) != m)

    far_out, far_in = ro.at[opp, :, :, window(q)], ri.at[q, :, :, window(q)]
    roots = [rcopy(far_out, far_in, ro_s.at[0], ro_r.at[0], opp)]
    for n, (to_rep, from_rep) in enumerate(((dn, up), (up, dn))):
        more = lanes(0, inner(opp))
        k = 1 + 7 * n
        roots.append(rcopy(ro.at[to_rep, n, :, more], ri.at[q, n, :, more], ro_s.at[k], ro_r.at[k], to_rep))
        for m in range(block // LANES):
            cols = pl.ds(m * LANES, LANES)
            k = 2 + 7 * n + m
            roots.append(
                rcopy(
                    ro.at[to_rep, :, :, cols], ri.at[q, :, :, cols], ro_s.at[k], ro_r.at[k], to_rep,
                    differs(m, to_rep, opp), differs(m, q, to_rep),
                )
            )
    roots_own = pltpu.make_async_copy(ro.at[q], ri.at[q], copy_sem.at[0])

    def start_roots():
        for copy in roots:
            copy.start()
        roots_own.start()

    first_sends(0)
    greet(near_sem, near)
    first_sends(1)
    pl.semaphore_wait(near_sem, len(near))
    greet(line_sem, further)
    loads[1].wait()
    loads[2].wait()
    for t in range(4):
        slot = stbl[lax.rem(t + 4 - my_shift, 4)]
        ro[t, 0] = rl_v[slot]
        ro[t, 1] = rr_v[slot]
    pl.semaphore_wait(line_sem, len(further))
    greet(plane_sem, x_line)
    for n in range(LAST + 1):
        relay_sums(n)
        if n + 2 <= LAST:
            first_sends(n + 2)
        if n == 0:
            pl.semaphore_wait(plane_sem, len(x_line))
            greet(cube_sem, y_line)
        if n >= 1:
            full_sums(n - 1)
            if n == 1:
                pl.semaphore_wait(cube_sem, len(y_line))
            send_pieces(n - 1)
    full_sums(LAST)
    send_pieces(LAST)
    start_roots()
    for n in range(len(CHUNKS)):
        await_block(a_r, n)

    def unpack_block(k, carry):
        c = lax.rem(k, 2)
        row0 = pl.multiple_of(k * TALL, 16)
        for t in range(4):
            G[pl.ds(row0, TALL), t * LANES : (t + 1) * LANES] = gi[t, k, 0:TALL, :]
        for t in range(2):
            into = slice((4 + t) * LANES, (5 + t) * LANES)
            G[pl.ds(row0, 32), into] = gi[t + 2 * c, k, TALL:PIECE, :]
            G[pl.ds(pl.multiple_of(row0 + 32, 16), 16), into] = gi[t + 2 * (1 - c), k, TALL:64, :]
        return carry

    lax.fori_loop(0, group, unpack_block, 0)

    def exchange(n):
        ss, rr = t_s.at[n], t_r.at[n]
        return [
            rcopy(to.at[n, opp], ti.at[n, q], ss.at[0], rr.at[0], opp),
            rcopy(to.at[n, up], ti.at[n, q], ss.at[1], rr.at[1], up),
            rcopy(to.at[n, dn], ti.at[n, q], ss.at[2], rr.at[2], dn),
        ], pltpu.make_async_copy(to.at[n, q], ti.at[n, q], copy_sem.at[1 + n])

    def products_left(c, carry):
        rows = G[pl.ds(pl.multiple_of(c * band, 16), band), :]
        to[0, c] = lax.dot_general(
            rows, G[...], (((1,), (1,)), ((), ())), preferred_element_type=F32
        ).astype(BF16)
        return carry

    def products_right(c, carry):
        rows = GT[pl.ds(pl.multiple_of(c * band, 16), band), :]
        to[1, c] = jnp.dot(rows, G[...], preferred_element_type=F32).astype(BF16)
        return carry

    stats = [exchange(n) for n in range(2)]

    def send_products(n):
        copies, own_copy = stats[n]
        for copy in copies:
            copy.start()
        own_copy.start()

    lax.fori_loop(0, 4, products_left, 0)
    send_products(0)
    GT[...] = G[...].T
    lax.fori_loop(0, 4, products_right, 0)

    send_products(1)
    await_all(roots, roots_own)
    for n, (x, y) in enumerate(((up, dn), (dn, up))):
        mine = lanes(0, inner(q))
        ri[:, n, :, mine] = ri[q, n, inner_rows(q), :].T.reshape(4, band, LANES)
        turned[:, 0:LANES] = ri[x, n, inner_rows(x), window(y)].T
        ri[y, n, :, lanes(0, inner(x))] = turned[pl.ds(pl.multiple_of(64 * lax.rem(y, 2), 16), band), 0:LANES]
        turned[...] = ri[:, n, :, window(opp)].reshape(block, 2 * LANES).T
        ri[opp, n] = turned[pl.ds(pl.multiple_of(64 * lax.rem(opp, 2), 16), band), :]

    per_band = band // TALL

    def precondition(b, carry):
        p = jnp.dot(ri[b, 0], G[...], preferred_element_type=F32).astype(BF16)
        u = jnp.dot(p, ri[:, 1].reshape(block, block), preferred_element_type=F32).astype(BF16)
        for n in range(per_band):
            k = b * per_band + n
            row0, c = n * TALL, n % 2
            for t in range(4):
                uo[t, k, 0:TALL, :] = u[row0 : row0 + TALL, t * LANES : (t + 1) * LANES]
            for t in range(2):
                part = u[row0 : row0 + TALL, (4 + t) * LANES : (5 + t) * LANES]
                uo[t + 2 * c, k, TALL:PIECE, :] = part[0:32]
                uo[t + 2 * (1 - c), k, TALL:64, :] = part[32:TALL]
        return carry

    lax.fori_loop(0, 4, precondition, 0)

    rb = (rb0, rb1, rb2)

    def send_back(n):
        row, count = CHUNKS[n]
        rows = pl.ds(row, count)

        def one(e, carry):
            if n < LAST:
                t, k = lax.rem(e, 4), lax.rem(e // 4 + fk, group)
            else:
                k = lax.rem(e // 2 + fk, group)
                t = 2 * lax.rem(k, 2) + lax.rem(e, 2)
            p = site_row * group + k
            copy = pltpu.make_async_remote_copy(
                src_ref=uo.at[t, k, rows], dst_ref=rb[n].at[f], send_sem=b_s.at[n], recv_sem=b_r.at[n],
                device_id=(p, t), device_id_type=MESH,
            )

            @pl.when(jnp.logical_not(jnp.logical_and(p == f, t == q)))
            def _():
                copy.start()

            return carry

        lax.fori_loop(0, nf if n < LAST else nf // 2, one, 0)

        @pl.when(own_row)
        def _():
            rb[n][f] = uo[q, fk, row : row + count]

    for n in range(len(CHUNKS)):
        send_back(n)

    def spread(n):
        row, count = CHUNKS[n]
        lo, hi, rows = pl.ds(0, half), pl.ds(half, half), pl.ds(row, count)
        if n < LAST:
            t_q = t_up = t_dn = t_opp = None
        else:
            t_q, t_up, t_dn, t_opp = tall_q, tall_up, tall_dn, tall_opp
        ss, rr = ag_s.at[n], ag_r.at[n]
        mine = ag.at[q, :, rows]
        from_up, from_dn = ag.at[up, lo, rows], ag.at[dn, hi, rows]
        return [
            rcopy(mine, mine, ss.at[0], rr.at[0], up, t_q, t_dn),
            rcopy(mine, mine, ss.at[1], rr.at[1], dn, t_q, t_up),
            rcopy(from_up, from_up, ss.at[2], rr.at[2], dn, t_up, t_opp),
            rcopy(from_dn, from_dn, ss.at[3], rr.at[3], up, t_dn, t_opp),
        ]

    gather = [spread(n) for n in range(len(CHUNKS))]

    def start_gather(n):
        row, count = CHUNKS[n]
        await_strip(b_r, n)

        def pick(j, carry):
            ag[q, j, row : row + count] = rb[n][own[fi, j]]
            return carry

        lax.fori_loop(0, bcols, pick, 0)
        gather[n][0].start()
        gather[n][1].start()

    def forward_gather(n):
        gather[n][1].wait_recv()
        gather[n][2].start()
        gather[n][0].wait_recv()
        gather[n][3].start()

    for n in range(LAST + 1):
        start_gather(n)
        if n >= 1:
            forward_gather(n - 1)
    forward_gather(LAST)

    for copies, own_copy in stats:
        await_all(copies, own_copy)
    for s in range(slots):
        decay[s] = jnp.where(slot_valid[s] > 0, jnp.float32(stat_decay), jnp.float32(1.0))
        for n in range(2):
            term = ti[n, lax.rem(slot_row[s] + my_shift, 4)]
            terms[n, s] = jnp.where(slot_valid[s] > 0, term, jnp.zeros_like(term))
    stores = [pltpu.make_async_copy(terms, terms_hbm, store_sem.at[0])] + [
        pltpu.make_async_copy(up_v.at[pl.ds(row, 16)], up_hbm.at[pl.ds(row, 16)], store_sem.at[1 + n])
        for n, row in enumerate((0, 32, 16))
    ]
    stores[0].start()

    def finish_gather(n):
        gather[n][2].wait_recv()
        gather[n][3].wait_recv()

        row, count = CHUNKS[n]
        end = row + count

        def unpack_row(j, carry):
            base = j * block
            if row < TALL:
                rows = slice(row, min(end, TALL))
                for t in range(4):
                    up_v[rows, lanes(base, t)] = ag[t, j, rows, :]
            for t in range(2):
                if row < 64 and end > TALL:
                    up_v[0:16, lanes(base, 4 + t)] = ag[t + 2 * core, j, TALL:64, :]
                    up_v[32:TALL, lanes(base, 4 + t)] = ag[t + 2 * (1 - core), j, TALL:64, :]
                if n == LAST:
                    up_v[16:32, lanes(base, 4 + t)] = ag[t + 2 * core, j, 64:PIECE, :]
            return carry

        lax.fori_loop(0, bcols, unpack_row, 0)

    for n in range(LAST):
        finish_gather(n)
    stores[1].start()
    stores[2].start()
    finish_gather(LAST)
    stores[3].start()

    for copies in rs + [roots, stats[0][0], stats[1][0]] + gather:
        for copy in copies:
            copy.wait_send()
    for n in range(len(CHUNKS)):
        await_strip(a_s, n)
        await_block(b_s, n)
    for store in stores:
        store.wait()


def shards(grads, owner_map, stats_left, stats_right, roots_left, roots_right):
    _, rows, width = grads.shape
    slots, band, block = stats_left.shape
    brows, bcols = owner_map.shape
    nf = lax.axis_size("fsdp")
    group = nf // brows
    half = bcols // 2
    parts = len(CHUNKS)
    dma, tally, reg = pltpu.SemaphoreType.DMA, pltpu.SemaphoreType.REGULAR, pltpu.VMEM
    msg = (PIECE, LANES)
    scratch = [
        reg((rows, width), BF16),
        reg((4, bcols) + msg, BF16),
        reg((2, half) + msg, BF16),
        reg((2, half) + msg, BF16),
        reg((2, half) + msg, BF16),
        reg((2, half) + msg, BF16),
        reg((bcols,) + msg, BF16),
        reg((nf,) + msg, BF16),
        reg((4, 2, band, block), BF16),
        reg((4, 2, band, block), BF16),
        reg((2 * LANES, block), BF16),
        reg((4, group) + msg, BF16),
        reg((block, block), BF16),
        reg((block, block), BF16),
        reg((4, group) + msg, BF16),
        *[reg((nf, count, LANES), BF16) for _, count in CHUNKS],
        reg((4, bcols) + msg, BF16),
        reg((2, 4, band, block), BF16),
        reg((2, 4, band, block), BF16),
        reg((2, slots, band, block), BF16),
        reg((slots, band, block), BF16),
        reg((slots, band, block), BF16),
        reg((rows, width), BF16),
        pltpu.SMEM((nf,), jnp.int32),
        pltpu.SMEM((brows,), jnp.int32),
        dma((3,)), dma((3,)), dma((4,)), tally, tally, tally, tally,
        dma((parts, 6)), dma((parts, 6)), dma((parts,)), dma((parts,)), dma((15,)), dma((15,)),
        dma((parts,)), dma((parts,)), dma((2, 3)), dma((2, 3)), dma((parts, 4)), dma((parts, 4)),
    ]
    hbm = pl.BlockSpec(memory_space=pl.ANY)
    decay, terms, update = pl.pallas_call(
        kernel,
        out_shape=(
            jax.ShapeDtypeStruct((slots,), F32),
            jax.ShapeDtypeStruct((2, slots, band, block), BF16),
            jax.ShapeDtypeStruct((rows, width), BF16),
        ),
        in_specs=[pl.BlockSpec(memory_space=pltpu.SMEM)] + [hbm] * 3,
        out_specs=(pl.BlockSpec(memory_space=pltpu.SMEM), hbm, hbm),
        scratch_shapes=scratch,
        compiler_params=pltpu.CompilerParams(
            collective_id=0, has_side_effects=True, vmem_limit_bytes=60 * 1024 * 1024
        ),
        name="shampoo",
    )(owner_map, grads, roots_left, roots_right)
    keep = decay[:, None, None]
    new_left = keep * stats_left + (1.0 - stat_decay) * terms[0].astype(F32)
    new_right = keep * stats_right + (1.0 - stat_decay) * terms[1].astype(F32)
    return new_left, new_right, update


def solution(mesh):
    in_specs = (
        P("rep", "fsdp", None),
        P(),
        P("fsdp", "rep", None),
        P("fsdp", "rep", None),
        P("fsdp", "rep", None),
        P("fsdp", "rep", None),
    )
    out_specs = (P("fsdp", "rep", None), P("fsdp", "rep", None), P("fsdp", None))
    return jax.shard_map(shards, mesh=mesh, in_specs=in_specs, out_specs=out_specs, check_vma=False)
```

```python
import jax
import jax.numpy as jnp
from jax import lax
from jax.experimental import pallas as pl
from jax.experimental.pallas import tpu as pltpu
from jax.sharding import PartitionSpec as P

stat_decay = 0.95
MESH = pl.DeviceIdType.MESH
LANES = 128
TALL = 48
PIECE = 80
CHUNKS = ((0, 32), (32, 32), (64, 16))
LAST = len(CHUNKS) - 1
BF16 = jnp.bfloat16
F32 = jnp.float32


class Copy:
    def __init__(self, copy, sends=None, receives=None):
        self.copy, self.sends, self.receives = copy, sends, receives

    def start(self):
        gated(self.sends, self.copy.start)

    def wait_send(self):
        gated(self.sends, self.copy.wait_send)

    def wait_recv(self):
        gated(self.receives, self.copy.wait_recv)


def gated(condition, act):
    if condition is None:
        act()
    else:

        @pl.when(condition)
        def _():
            act()


def kernel(
    own, g_hbm, rl_hbm, rr_hbm,
    decay, terms_hbm, up_hbm,
    g_v, pk, rs_rel, rs_dir, rs_acc, rs_out, strip,
    out, ro, ri, turned, gi, G, GT,
    uo, rb0, rb1, rb2, ag, to, ti, terms,
    rl_v, rr_v, up_v, jtbl, stbl,
    load_sem, copy_sem, store_sem, near_sem, line_sem, plane_sem, cube_sem,
    rs_s, rs_r, a_s, a_r, ro_s, ro_r, b_s, b_r, t_s, t_r, ag_s, ag_r,
):
    f = lax.axis_index("fsdp")
    q = lax.axis_index("rep")
    nf = lax.axis_size("fsdp")
    brows, bcols = own.shape
    group = nf // brows
    block = G.shape[0]
    slots, band, _ = rl_v.shape
    half = bcols // 2
    up, dn, opp = lax.rem(q + 1, 4), lax.rem(q + 3, 4), lax.rem(q + 2, 4)
    fi, fk, core = f // group, lax.rem(f, group), lax.rem(f, 2)

    def rcopy(src, dst, ssem, rsem, rep, sends=None, receives=None):
        copy = pltpu.make_async_remote_copy(
            src_ref=src, dst_ref=dst, send_sem=ssem, recv_sem=rsem,
            device_id=(f, rep), device_id_type=MESH,
        )
        return Copy(copy, sends, receives)

    loads = [
        pltpu.make_async_copy(src, dst, load_sem.at[n])
        for n, (src, dst) in enumerate(
            [(g_hbm.at[0], g_v), (rl_hbm, rl_v), (rr_hbm, rr_v)]
        )
    ]

    def shift(o):
        return lax.rem(2 * lax.rem(o, 2) + lax.rem(o // 2, 4) + o // 8, 4)

    my_shift = shift(f)
    site_row = lax.rem(q + 4 - my_shift, 4)
    own_row = site_row == fi

    def along_z(n):
        return (lax.rem(f + 8 * n, nf), q)

    def along_x(n):
        return ((f // 8) * 8 + lax.rem(f + n, 8), q)

    near = [along_z(1), along_z(7), along_x(1), along_x(7)]
    further = [along_z(2), along_z(6), along_x(2), along_x(6)]
    x_line = [along_x(n) for n in range(1, 8)]
    y_line = [(f, up), (f, dn), (f, opp)]

    def greet(sem, devices):
        for device in devices:
            pl.semaphore_signal(sem, inc=1, device_id=device, device_id_type=MESH)

    loads[0].start()
    barrier = pltpu.get_barrier_semaphore()
    greet(barrier, y_line + near)
    for load in loads[1:]:
        load.start()

    def column_of(o, carry):
        col = jnp.int32(0)
        for j in range(bcols):
            col = jnp.where(own[fi, j] == o, jnp.int32(j), col)
        jtbl[o] = col
        return carry

    lax.fori_loop(0, nf, column_of, 0)
    held = []
    for t in range(brows):
        count = jnp.int32(0)
        for j in range(bcols):
            count = count + jnp.where(own[t, j] == f, jnp.int32(1), jnp.int32(0))
        held.append(count)
    before = jnp.int32(0)
    for t in range(brows):
        stbl[t] = jnp.minimum(before, slots - 1)
        before = before + held[t]
    slot_row, slot_valid = [], []
    for s in range(slots):
        row, valid = jnp.int32(0), jnp.int32(0)
        before = jnp.int32(0)
        for t in range(brows):
            hit = jnp.where(before == s, held[t], 0)
            row = row + hit * t
            valid = valid + hit
            before = before + held[t]
        slot_row.append(row)
        slot_valid.append(valid)

    def tall(t, c):
        return lax.rem(t + 2 * c, 4) < 2

    tall_q, tall_up, tall_dn, tall_opp = [tall(t, core) for t in (q, up, dn, opp)]

    def lanes(base, group_of):
        return pl.ds(pl.multiple_of(base + group_of * LANES, LANES), LANES)

    loads[0].wait()

    def pack(j, carry):
        base = j * block
        for t in range(4):
            pk[t, j, 0:TALL, :] = g_v[:, lanes(base, t)]
        for t in range(2):
            pk[t + 2 * core, j, TALL:PIECE, :] = g_v[0:32, lanes(base, 4 + t)]
            pk[t + 2 * (1 - core), j, TALL:64, :] = g_v[32:TALL, lanes(base, 4 + t)]
        return carry

    lax.fori_loop(0, bcols, pack, 0)
    pl.semaphore_wait(barrier, len(y_line) + len(near))

    def sums(n):
        row, count = CHUNKS[n]
        lo, hi, rows = pl.ds(0, half), pl.ds(half, half), pl.ds(row, count)
        if n < LAST:
            s_up = s_dn = s_opp = r_up = r_dn = r_q = None
        else:
            s_up, s_dn, s_opp, r_up, r_dn, r_q = tall_up, tall_dn, tall_opp, tall_up, tall_dn, tall_q
        ss, rr = rs_s.at[n], rs_r.at[n]
        return [
            rcopy(pk.at[opp, lo, rows], rs_rel.at[0, :, rows], ss.at[0], rr.at[0], dn, s_opp, r_dn),
            rcopy(pk.at[opp, hi, rows], rs_rel.at[1, :, rows], ss.at[1], rr.at[1], up, s_opp, r_up),
            rcopy(pk.at[up, lo, rows], rs_dir.at[0, :, rows], ss.at[2], rr.at[2], up, s_up, r_q),
            rcopy(pk.at[dn, hi, rows], rs_dir.at[1, :, rows], ss.at[3], rr.at[3], dn, s_dn, r_q),
            rcopy(rs_out.at[0, :, rows], rs_acc.at[0, :, rows], ss.at[4], rr.at[4], dn, s_dn, r_q),
            rcopy(rs_out.at[1, :, rows], rs_acc.at[1, :, rows], ss.at[5], rr.at[5], up, s_up, r_q),
        ]

    rs = [sums(n) for n in range(len(CHUNKS))]

    def first_sends(n):
        for copy in rs[n][:4]:
            copy.start()

    def relay_sums(n):
        row, count = CHUNKS[n]
        rows = slice(row, row + count)
        for side, first, target in ((0, 0, dn), (1, half, up)):
            rs[n][side].wait_recv()

            def body(j, carry):
                total = rs_rel[side, j, rows].astype(F32) + pk[target, first + j, rows].astype(F32)
                rs_out[side, j, rows] = total.astype(BF16)
                return carry

            lax.fori_loop(0, half, body, 0)
            rs[n][4 + side].start()

    def full_sums(n):
        row, count = CHUNKS[n]
        rows = slice(row, row + count)
        for side, first in ((0, 0), (1, half)):
            rs[n][2 + side].wait_recv()
            rs[n][4 + side].wait_recv()

            def body(j, carry):
                total = pk[q, first + j, rows].astype(F32) + rs_dir[side, j, rows].astype(F32)
                strip[first + j, rows] = (total + rs_acc[side, j, rows].astype(F32)).astype(BF16)
                return carry

            lax.fori_loop(0, half, body, 0)

    def send_pieces(n):
        row, count = CHUNKS[n]
        rows = pl.ds(row, count)

        def piece_copy(o):
            return pltpu.make_async_remote_copy(
                src_ref=out.at[o, rows], dst_ref=gi.at[q, fk, rows], send_sem=a_s.at[n], recv_sem=a_r.at[n],
                device_id=(o, lax.rem(fi + shift(o), 4)), device_id_type=MESH,
            )

        def send_piece(d, carry):
            o = lax.rem(f + d, nf)
            out[o, row : row + count] = strip[jtbl[o], row : row + count]
            piece_copy(o).start()
            return carry

        def send_all():
            lax.fori_loop(1, nf, send_piece, 0)

            @pl.when(own_row)
            def _():
                gi[q, fk, row : row + count] = strip[jtbl[f], row : row + count]

            @pl.when(jnp.logical_not(own_row))
            def _():
                out[f, row : row + count] = strip[jtbl[f], row : row + count]
                piece_copy(f).start()

        gated(None if n < LAST else tall_q, send_all)

    def await_pieces(sem, n, total, here):
        count = CHUNKS[n][1]

        def some(pieces):
            view = out.at[pl.ds(0, pieces), pl.ds(0, count)]
            pltpu.make_async_copy(view, view, sem.at[n]).wait()

        pl.when(here)(lambda: some(total - 1))
        pl.when(jnp.logical_not(here))(lambda: some(total))

    def await_strip(sem, n):
        gated(None if n < LAST else tall_q, lambda: await_pieces(sem, n, nf, own_row))

    def await_block(sem, n):
        if n < LAST:
            await_pieces(sem, n, nf, own_row)
        else:
            await_pieces(sem, n, nf // 2, jnp.logical_and(own_row, tall_q))

    def await_all(copies, own_copy):
        for copy in copies:
            copy.wait_recv()
        own_copy.wait()

    def window(t):
        return pl.ds(pl.multiple_of(LANES * (t + t // 2), LANES), 2 * LANES)

    def inner(t):
        return (3 * t + 1) // 2

    def inner_rows(t):
        return pl.ds(pl.multiple_of(64 * lax.rem(t, 2), 16), LANES)

    def differs(m, t, u):
        return jnp.logical_and(inner(t) != m, inner(u) != m)

    def corner_rows(t):
        return pl.ds(pl.multiple_of(LANES * (1 - lax.rem(t, 2)), 16), 64)

    def corner_lanes(t):
        return lanes(0, t + t // 2 + 1 - lax.rem(t, 2))

    far = [(pl.ds(0, band), lanes(0, inner(q))), (corner_rows(q), corner_lanes(q))]
    roots = [
        rcopy(ro.at[opp, :, rows, cols], ri.at[q, :, rows, cols], ro_s.at[k], ro_r.at[k], opp)
        for k, (rows, cols) in zip((0, 15), far)
    ]
    for n, (to_rep, from_rep) in enumerate(((dn, up), (up, dn))):
        more = lanes(0, inner(opp))
        k = 1 + 7 * n
        roots.append(rcopy(ro.at[to_rep, n, :, more], ri.at[q, n, :, more], ro_s.at[k], ro_r.at[k], to_rep))
        for m in range(block // LANES):
            cols = pl.ds(m * LANES, LANES)
            k = 2 + 7 * n + m
            roots.append(
                rcopy(
                    ro.at[to_rep, :, :, cols], ri.at[q, :, :, cols], ro_s.at[k], ro_r.at[k], to_rep,
                    differs(m, to_rep, opp), differs(m, q, to_rep),
                )
            )
    roots_own = pltpu.make_async_copy(ro.at[q], ri.at[q], copy_sem.at[0])

    def start_roots():
        for copy in roots:
            copy.start()
        roots_own.start()

    first_sends(0)
    greet(near_sem, near)
    first_sends(1)
    pl.semaphore_wait(near_sem, len(near))
    greet(line_sem, further)
    loads[1].wait()
    loads[2].wait()
    for t in range(4):
        slot = stbl[lax.rem(t + 4 - my_shift, 4)]
        ro[t, 0] = rl_v[slot]
        ro[t, 1] = rr_v[slot]
    pl.semaphore_wait(line_sem, len(further))
    greet(plane_sem, x_line)
    for n in range(LAST + 1):
        relay_sums(n)
        if n + 2 <= LAST:
            first_sends(n + 2)
        if n == 0:
            pl.semaphore_wait(plane_sem, len(x_line))
            greet(cube_sem, y_line)
        if n >= 1:
            full_sums(n - 1)
            if n == 1:
                pl.semaphore_wait(cube_sem, len(y_line))
            send_pieces(n - 1)
    full_sums(LAST)
    send_pieces(LAST)
    start_roots()
    for n in range(len(CHUNKS)):
        await_block(a_r, n)

    def unpack_block(k, carry):
        c = lax.rem(k, 2)
        row0 = pl.multiple_of(k * TALL, 16)
        for t in range(4):
            G[pl.ds(row0, TALL), t * LANES : (t + 1) * LANES] = gi[t, k, 0:TALL, :]
        for t in range(2):
            into = slice((4 + t) * LANES, (5 + t) * LANES)
            G[pl.ds(row0, 32), into] = gi[t + 2 * c, k, TALL:PIECE, :]
            G[pl.ds(pl.multiple_of(row0 + 32, 16), 16), into] = gi[t + 2 * (1 - c), k, TALL:64, :]
        return carry

    lax.fori_loop(0, group, unpack_block, 0)

    def exchange(n):
        ss, rr = t_s.at[n], t_r.at[n]
        return [
            rcopy(to.at[n, opp], ti.at[n, q], ss.at[0], rr.at[0], opp),
            rcopy(to.at[n, up], ti.at[n, q], ss.at[1], rr.at[1], up),
            rcopy(to.at[n, dn], ti.at[n, q], ss.at[2], rr.at[2], dn),
        ], pltpu.make_async_copy(to.at[n, q], ti.at[n, q], copy_sem.at[1 + n])

    def products_left(c, carry):
        rows = G[pl.ds(pl.multiple_of(c * band, 16), band), :]
        to[0, c] = lax.dot_general(
            rows, G[...], (((1,), (1,)), ((), ())), preferred_element_type=F32
        ).astype(BF16)
        return carry

    def products_right(c, carry):
        rows = GT[pl.ds(pl.multiple_of(c * band, 16), band), :]
        to[1, c] = jnp.dot(rows, G[...], preferred_element_type=F32).astype(BF16)
        return carry

    stats = [exchange(n) for n in range(2)]

    def send_products(n):
        copies, own_copy = stats[n]
        for copy in copies:
            copy.start()
        own_copy.start()

    lax.fori_loop(0, 4, products_left, 0)
    send_products(0)
    GT[...] = G[...].T
    lax.fori_loop(0, 4, products_right, 0)

    send_products(1)
    await_all(roots, roots_own)
    for n, (x, y) in enumerate(((up, dn), (dn, up))):
        mine = lanes(0, inner(q))
        ri[:, n, :, mine] = ri[q, n, inner_rows(q), :].T.reshape(4, band, LANES)
        turned[:, 0:LANES] = ri[x, n, inner_rows(x), window(y)].T
        ri[y, n, :, lanes(0, inner(x))] = turned[pl.ds(pl.multiple_of(64 * lax.rem(y, 2), 16), band), 0:LANES]
        edge = ri[opp, n, corner_rows(opp), lanes(0, inner(opp))]
        ri[opp, n, inner_rows(opp), corner_lanes(opp)] = jnp.concatenate([edge, edge], axis=0).T
        turned[...] = ri[:, n, :, window(opp)].reshape(block, 2 * LANES).T
        ri[opp, n] = turned[pl.ds(pl.multiple_of(64 * lax.rem(opp, 2), 16), band), :]

    per_band = band // TALL

    def precondition(b, carry):
        p = jnp.dot(ri[b, 0], G[...], preferred_element_type=F32).astype(BF16)
        u = jnp.dot(p, ri[:, 1].reshape(block, block), preferred_element_type=F32).astype(BF16)
        for n in range(per_band):
            k = b * per_band + n
            row0, c = n * TALL, n % 2
            for t in range(4):
                uo[t, k, 0:TALL, :] = u[row0 : row0 + TALL, t * LANES : (t + 1) * LANES]
            for t in range(2):
                part = u[row0 : row0 + TALL, (4 + t) * LANES : (5 + t) * LANES]
                uo[t + 2 * c, k, TALL:PIECE, :] = part[0:32]
                uo[t + 2 * (1 - c), k, TALL:64, :] = part[32:TALL]
        return carry

    lax.fori_loop(0, 4, precondition, 0)

    rb = (rb0, rb1, rb2)

    def send_back(n):
        row, count = CHUNKS[n]
        rows = pl.ds(row, count)

        def one(e, carry):
            if n < LAST:
                t, k = lax.rem(e, 4), lax.rem(e // 4 + fk, group)
            else:
                k = lax.rem(e // 2 + fk, group)
                t = 2 * lax.rem(k, 2) + lax.rem(e, 2)
            p = site_row * group + k
            copy = pltpu.make_async_remote_copy(
                src_ref=uo.at[t, k, rows], dst_ref=rb[n].at[f], send_sem=b_s.at[n], recv_sem=b_r.at[n],
                device_id=(p, t), device_id_type=MESH,
            )

            @pl.when(jnp.logical_not(jnp.logical_and(p == f, t == q)))
            def _():
                copy.start()

            return carry

        lax.fori_loop(0, nf if n < LAST else nf // 2, one, 0)

        @pl.when(own_row)
        def _():
            rb[n][f] = uo[q, fk, row : row + count]

    for n in range(len(CHUNKS)):
        send_back(n)

    def spread(n):
        row, count = CHUNKS[n]
        lo, hi, rows = pl.ds(0, half), pl.ds(half, half), pl.ds(row, count)
        if n < LAST:
            t_q = t_up = t_dn = t_opp = None
        else:
            t_q, t_up, t_dn, t_opp = tall_q, tall_up, tall_dn, tall_opp
        ss, rr = ag_s.at[n], ag_r.at[n]
        mine = ag.at[q, :, rows]
        from_up, from_dn = ag.at[up, lo, rows], ag.at[dn, hi, rows]
        return [
            rcopy(mine, mine, ss.at[0], rr.at[0], up, t_q, t_dn),
            rcopy(mine, mine, ss.at[1], rr.at[1], dn, t_q, t_up),
            rcopy(from_up, from_up, ss.at[2], rr.at[2], dn, t_up, t_opp),
            rcopy(from_dn, from_dn, ss.at[3], rr.at[3], up, t_dn, t_opp),
        ]

    gather = [spread(n) for n in range(len(CHUNKS))]

    def start_gather(n):
        row, count = CHUNKS[n]
        await_strip(b_r, n)

        def pick(j, carry):
            ag[q, j, row : row + count] = rb[n][own[fi, j]]
            return carry

        lax.fori_loop(0, bcols, pick, 0)
        gather[n][0].start()
        gather[n][1].start()

    def forward_gather(n):
        gather[n][1].wait_recv()
        gather[n][2].start()
        gather[n][0].wait_recv()
        gather[n][3].start()

    for n in range(LAST + 1):
        start_gather(n)
        if n >= 1:
            forward_gather(n - 1)
    forward_gather(LAST)

    for copies, own_copy in stats:
        await_all(copies, own_copy)
    for s in range(slots):
        decay[s] = jnp.where(slot_valid[s] > 0, jnp.float32(stat_decay), jnp.float32(1.0))
        for n in range(2):
            term = ti[n, lax.rem(slot_row[s] + my_shift, 4)]
            terms[n, s] = jnp.where(slot_valid[s] > 0, term, jnp.zeros_like(term))
    stores = [pltpu.make_async_copy(terms, terms_hbm, store_sem.at[0])] + [
        pltpu.make_async_copy(up_v.at[pl.ds(row, 16)], up_hbm.at[pl.ds(row, 16)], store_sem.at[1 + n])
        for n, row in enumerate((0, 32, 16))
    ]
    stores[0].start()

    def finish_gather(n):
        gather[n][2].wait_recv()
        gather[n][3].wait_recv()

        row, count = CHUNKS[n]
        end = row + count

        def unpack_row(j, carry):
            base = j * block
            if row < TALL:
                rows = slice(row, min(end, TALL))
                for t in range(4):
                    up_v[rows, lanes(base, t)] = ag[t, j, rows, :]
            for t in range(2):
                if row < 64 and end > TALL:
                    up_v[0:16, lanes(base, 4 + t)] = ag[t + 2 * core, j, TALL:64, :]
                    up_v[32:TALL, lanes(base, 4 + t)] = ag[t + 2 * (1 - core), j, TALL:64, :]
                if n == LAST:
                    up_v[16:32, lanes(base, 4 + t)] = ag[t + 2 * core, j, 64:PIECE, :]
            return carry

        lax.fori_loop(0, bcols, unpack_row, 0)

    for n in range(LAST):
        finish_gather(n)
    stores[1].start()
    stores[2].start()
    finish_gather(LAST)
    stores[3].start()

    for copies in rs + [roots, stats[0][0], stats[1][0]] + gather:
        for copy in copies:
            copy.wait_send()
    for n in range(len(CHUNKS)):
        await_strip(a_s, n)
        await_block(b_s, n)
    for store in stores:
        store.wait()


def shards(grads, owner_map, stats_left, stats_right, roots_left, roots_right):
    _, rows, width = grads.shape
    slots, band, block = stats_left.shape
    brows, bcols = owner_map.shape
    nf = lax.axis_size("fsdp")
    group = nf // brows
    half = bcols // 2
    parts = len(CHUNKS)
    dma, tally, reg = pltpu.SemaphoreType.DMA, pltpu.SemaphoreType.REGULAR, pltpu.VMEM
    msg = (PIECE, LANES)
    scratch = [
        reg((rows, width), BF16),
        reg((4, bcols) + msg, BF16),
        reg((2, half) + msg, BF16),
        reg((2, half) + msg, BF16),
        reg((2, half) + msg, BF16),
        reg((2, half) + msg, BF16),
        reg((bcols,) + msg, BF16),
        reg((nf,) + msg, BF16),
        reg((4, 2, band, block), BF16),
        reg((4, 2, band, block), BF16),
        reg((2 * LANES, block), BF16),
        reg((4, group) + msg, BF16),
        reg((block, block), BF16),
        reg((block, block), BF16),
        reg((4, group) + msg, BF16),
        *[reg((nf, count, LANES), BF16) for _, count in CHUNKS],
        reg((4, bcols) + msg, BF16),
        reg((2, 4, band, block), BF16),
        reg((2, 4, band, block), BF16),
        reg((2, slots, band, block), BF16),
        reg((slots, band, block), BF16),
        reg((slots, band, block), BF16),
        reg((rows, width), BF16),
        pltpu.SMEM((nf,), jnp.int32),
        pltpu.SMEM((brows,), jnp.int32),
        dma((3,)), dma((3,)), dma((4,)), tally, tally, tally, tally,
        dma((parts, 6)), dma((parts, 6)), dma((parts,)), dma((parts,)), dma((16,)), dma((16,)),
        dma((parts,)), dma((parts,)), dma((2, 3)), dma((2, 3)), dma((parts, 4)), dma((parts, 4)),
    ]
    hbm = pl.BlockSpec(memory_space=pl.ANY)
    decay, terms, update = pl.pallas_call(
        kernel,
        out_shape=(
            jax.ShapeDtypeStruct((slots,), F32),
            jax.ShapeDtypeStruct((2, slots, band, block), BF16),
            jax.ShapeDtypeStruct((rows, width), BF16),
        ),
        in_specs=[pl.BlockSpec(memory_space=pltpu.SMEM)] + [hbm] * 3,
        out_specs=(pl.BlockSpec(memory_space=pltpu.SMEM), hbm, hbm),
        scratch_shapes=scratch,
        compiler_params=pltpu.CompilerParams(
            collective_id=0, has_side_effects=True, vmem_limit_bytes=60 * 1024 * 1024
        ),
        name="shampoo",
    )(owner_map, grads, roots_left, roots_right)
    keep = decay[:, None, None]
    new_left = keep * stats_left + (1.0 - stat_decay) * terms[0].astype(F32)
    new_right = keep * stats_right + (1.0 - stat_decay) * terms[1].astype(F32)
    return new_left, new_right, update


def solution(mesh):
    in_specs = (
        P("rep", "fsdp", None),
        P(),
        P("fsdp", "rep", None),
        P("fsdp", "rep", None),
        P("fsdp", "rep", None),
        P("fsdp", "rep", None),
    )
    out_specs = (P("fsdp", "rep", None), P("fsdp", "rep", None), P("fsdp", None))
    return jax.shard_map(shards, mesh=mesh, in_specs=in_specs, out_specs=out_specs, check_vma=False)
```
